512 devices in a mesh: dp: 16 (over x, z_hi), pipe: 8 (over y, core), tensor: 4 (over z_lo).
Axes of the slice: x: 4, y: 4, z: 16 (z_hi: 4, z_lo: 4; z = z_hi * 4 + z_lo), core: 2. Of those that a mesh axis runs over, the one named last changes fastest.
Arguments:
- section_input: bfloat16 [8, 2048, 4096], P('pipe', 'dp'), may hold values from -60 to 60
- out_grad: bfloat16 [8, 2048, 4096], P('pipe', 'dp'), may hold values from -1 to 1
- head_grad: bfloat16 [8, 2048, 2048], P('pipe', 'dp', 'tensor'), may hold values from -8 to 8
- encoder: bfloat16 [2048, 4096], P(('dp', 'pipe', 'tensor')), may hold values from -12 to 12
- norm_gain: float32 [8, 4096], P('pipe'), may hold values from 0.25 to 1.75
- query_weight: bfloat16 [8, 4096, 2048], P('pipe', 'dp', 'tensor'), may hold values from -0.09375 to 0.09375
- key_weight: bfloat16 [8, 4096, 2048], P('pipe', 'dp', 'tensor'), may hold values from -0.09375 to 0.09375
- value_weight: bfloat16 [8, 4096, 2048], P('pipe', 'dp', 'tensor'), may hold values from -0.09375 to 0.09375
Outputs:
- input_grad: bfloat16 [8, 2048, 4096], P('pipe', 'dp', 'tensor')
- encoder_grad: float32 [2048, 4096], P(('dp', 'pipe', 'tensor'))
- gain_grad: float32 [8, 4096], P('pipe', 'tensor')
The draws below stay inside these ranges and needn't reach their ends.
All inputs are finite; a program needn't handle non-finite values.
Results may differ from the reference program's by a relative error of at most 0.03.
Values may be sent and summed in bfloat16 or wider, within the bound.
A program may use at most 64 MiB of HBM per device.

```python
import math
import jax
import jax.numpy as jnp
from jax import lax

D = 4096
HEADS = 8
HEAD_DIM = 256
TGT = 128
SRC = 128
LAYERS = 8
BATCH = 16
TOKENS = 2048
ENC_ROWS = 2048
HC = 2048
N_TENSOR = 4


def draw_section_input(key, part):
    key = jax.random.fold_in(key, 11)
    first, second, third = jax.random.split(key, 3)
    shape = (LAYERS, TOKENS, D)
    row_scale = jnp.exp(jax.random.uniform(second, (LAYERS, TOKENS, 1), minval=math.log(0.3), maxval=math.log(3.0)))
    col_scale = jnp.exp(jax.random.uniform(third, (LAYERS, 1, D), minval=math.log(0.4), maxval=math.log(4.0)))
    values = jnp.clip(jax.random.normal(first, shape), -5.0, 5.0)
    return (values * row_scale * col_scale).astype(jnp.bfloat16)


def rising_values(key, shape, amplitude):
    sequence = (jnp.arange(TOKENS) // TGT).astype(jnp.float32).reshape(1, TOKENS, 1)
    rising = sequence / max(BATCH - 1, 1)
    values = jnp.clip(jax.random.normal(key, shape), -5.0, 5.0)
    scale = 0.5 * amplitude * 3.0 ** rising
    return values * scale


def draw_out_grad(key, part):
    key = jax.random.fold_in(key, 23)
    return rising_values(key, (LAYERS, TOKENS, D), 0.1).astype(jnp.bfloat16)


def draw_head_grad(key, part):
    key = jax.random.fold_in(key, 37)
    return rising_values(key, (LAYERS, TOKENS, HC), 1.0).astype(jnp.bfloat16)


def block_scale(stream_key, shape, shards, least, top_value):
    loudness, own = 1.0, jax.random.fold_in(stream_key, 6)
    for dim, parts in shards:
        steps = jnp.exp(jax.random.uniform(jax.random.fold_in(own, dim), (parts,), jnp.float32, least / len(shards), top_value / len(shards)))
        loudness = loudness * jnp.repeat(steps, shape[dim] // parts).reshape([-1 if axis == dim else 1 for axis in range(len(shape))])
    return loudness


def scatter_about(own_key, dims, width, limit, shards=(), held_as=jnp.bfloat16):
    result = width * jax.random.normal(own_key, dims, jnp.float32)
    if shards:
        result = result * block_scale(own_key, dims, shards, -0.22, 0.18)
    return jnp.clip(result, -limit, limit).astype(held_as)


def setup_inputs(seed: int = 0) -> dict:
    keys = jax.random.split(jax.random.key(seed), 9)
    return {
        "section_input": draw_section_input(jax.random.fold_in(keys[8], 71), 0),
        "out_grad": draw_out_grad(jax.random.fold_in(keys[8], 71), 0),
        "head_grad": draw_head_grad(jax.random.fold_in(keys[8], 71), 0),
        "encoder": scatter_about(keys[3], (ENC_ROWS, D), 2.0, 12.0, ((0, 512),)),
        "norm_gain": jnp.clip(1.0 + 0.15 * jax.random.normal(keys[4], (LAYERS, D), jnp.float32), 0.25, 1.75),
        "query_weight": scatter_about(keys[5], (LAYERS, D, HC), D ** -0.5, 0.09375, ((0, 8), (1, 16), (2, 4))),
        "key_weight": scatter_about(keys[6], (LAYERS, D, HC), D ** -0.5, 0.09375, ((0, 8), (1, 16), (2, 4))),
        "value_weight": scatter_about(keys[7], (LAYERS, D, HC), D ** -0.5, 0.09375, ((0, 8), (1, 16), (2, 4))),
    }


EPSILON = 1e-06

def contract_last(left, right):
    return lax.dot_general(left, right, (((1,), (1,)), ((), ())), preferred_element_type=jnp.float32)

def layer_grads(stream, upstream, head_cot, gains, w_query, w_key, w_value, encoder):
    stream_f = stream.astype(jnp.float32)
    inv_rms = lax.rsqrt(lax.optimization_barrier(jnp.mean(stream_f * stream_f, axis=-1, keepdims=True)) + EPSILON)
    normed = stream_f * inv_rms
    hidden = (normed * gains).astype(jnp.bfloat16)
    queries = jnp.dot(hidden, w_query, preferred_element_type=jnp.float32).astype(jnp.bfloat16)
    keys_all = jnp.dot(encoder, w_key, preferred_element_type=jnp.float32).astype(jnp.bfloat16)
    values_all = jnp.dot(encoder, w_value, preferred_element_type=jnp.float32).astype(jnp.bfloat16)
    head_scale = 1.0 / math.sqrt(HEAD_DIM)
    q_heads = queries.astype(jnp.float32).reshape(BATCH, TGT, HEADS, HEAD_DIM)
    k_heads = keys_all.astype(jnp.float32).reshape(BATCH, SRC, HEADS, HEAD_DIM)
    v_heads = values_all.astype(jnp.float32).reshape(BATCH, SRC, HEADS, HEAD_DIM)
    scores = jnp.einsum('bqhd,bkhd->bhqk', q_heads, k_heads) * head_scale
    expo = jnp.exp(scores)
    probs = expo / lax.optimization_barrier(jnp.sum(expo, axis=-1, keepdims=True))
    probs_low = lax.optimization_barrier(probs.astype(jnp.bfloat16)).astype(jnp.float32)
    a_heads = head_cot.astype(jnp.float32).reshape(BATCH, TGT, HEADS, HEAD_DIM)
    prob_grad = jnp.einsum('bqhd,bkhd->bhqk', a_heads, v_heads)
    score_grad = (probs * (prob_grad - lax.optimization_barrier(jnp.sum(prob_grad * probs, axis=-1, keepdims=True))) * head_scale).astype(jnp.bfloat16)
    score_f = lax.optimization_barrier(score_grad).astype(jnp.float32)
    query_grad = jnp.einsum('bhqk,bkhd->bqhd', score_f, k_heads).astype(jnp.bfloat16).reshape(TOKENS, HC)
    key_grad = jnp.einsum('bhqk,bqhd->bkhd', score_f, q_heads).astype(jnp.bfloat16).reshape(ENC_ROWS, HC)
    value_grad = jnp.einsum('bhqk,bqhd->bkhd', probs_low, a_heads).astype(jnp.bfloat16).reshape(ENC_ROWS, HC)
    group_cols = HC // N_TENSOR
    grouped_q = query_grad.astype(jnp.float32).reshape(TOKENS, N_TENSOR, group_cols)
    grouped_w = w_query.astype(jnp.float32).reshape(D, N_TENSOR, group_cols)
    partials = jnp.einsum('tgc,dgc->gtd', grouped_q, grouped_w).astype(jnp.bfloat16)
    hidden_grad = lax.optimization_barrier(jnp.sum(lax.optimization_barrier(partials).astype(jnp.float32), axis=0))
    normed_grad = hidden_grad * gains
    inner = lax.optimization_barrier(jnp.mean(normed_grad * normed, axis=-1, keepdims=True))
    input_grad = (upstream.astype(jnp.float32) + inv_rms * (normed_grad - normed * inner)).astype(jnp.bfloat16)
    gain_grad = lax.optimization_barrier(jnp.sum(hidden_grad * normed, axis=0))
    encoder_grad = contract_last(key_grad, w_key) + contract_last(value_grad, w_value)
    return (input_grad, gain_grad, encoder_grad)

def reference(section_input, out_grad, head_grad, encoder, norm_gain, query_weight, key_weight, value_weight):

    def layer_step(running, layer):
        stream, upstream, head_cot, gains, w_query, w_key, w_value = layer
        input_grad, gain_grad, encoder_grad = layer_grads(stream, upstream, head_cot, gains, w_query, w_key, w_value, encoder)
        return (running + encoder_grad, (input_grad, gain_grad))
    running, (input_grads, gain_grads) = lax.scan(layer_step, jnp.zeros((ENC_ROWS, D), jnp.float32), (section_input, out_grad, head_grad, norm_gain, query_weight, key_weight, value_weight))
    return (input_grads, running, gain_grads)
```

```python
import functools
import math

import jax
import jax.numpy as jnp
from jax import lax
from jax.experimental import pallas as pl
from jax.experimental.pallas import tpu as pltpu
from jax.sharding import PartitionSpec as P

HEAD_DIM = 256
HEADS_HERE = 2
COLS = 512
D = 4096
ROWS = 128
SHARD = 256
BLOCK = 1024
EPSILON = 1e-06

SUBS = 4
CHUNK = SHARD // SUBS
HALF = CHUNK // 2
CHUNKS = 3 * SUBS
Z_AHEAD = 2
X_AHEAD = 4
MESH = pl.DeviceIdType.MESH


def dot_nt(left, right):
    return lax.dot_general(
        left, right, (((1,), (1,)), ((), ())), preferred_element_type=jnp.float32
    )


def dot_tn(left, right):
    return lax.dot_general(
        left, right, (((0,), (0,)), ((), ())), preferred_element_type=jnp.float32
    )


def regroup(rows):
    i = lax.broadcasted_iota(jnp.int32, (64, 64), 0)
    j = lax.broadcasted_iota(jnp.int32, (64, 64), 1)
    source = (i % 16) // 4 * 16 + i // 16 * 4 + i % 4
    hot = jnp.where(j == source, 1.0, 0.0).astype(jnp.bfloat16)
    return jnp.dot(hot, rows, preferred_element_type=jnp.float32)


def kernel(
    x_hbm, og_hbm, hg_hbm, enc_hbm, gain_ref, wq_hbm, wk_hbm, wv_hbm,
    ig_ref, eg_ref, gg_ref,
    w, xv, og, hg, enc64, enc, hid, inv, acc, qb, kb, vb, dq, dk, dv,
    hp, hp_in, inner, de, de1, de1_in, de2, de2_in, de3, de3_in, gz, gx,
    local, z_send, x_send, z_near, z_far, x_near, x_far,
    e_send, e_recv, h_send, h_recv, i_send, i_recv, d_send, d_recv, g_send, g_recv,
):
    dp = lax.axis_index("dp")
    pipe = lax.axis_index("pipe")
    t = lax.axis_index("tensor")
    x, z = dp // 4, dp % 4
    y, core = pipe // 2, pipe % 2

    def at_z(k):
        return (x * 4 + (z + k) % 4, pipe, t)

    def at_x(k):
        return ((x + k) % 4 * 4 + z, pipe, t)

    def at_y(k):
        return (dp, (y + k) % 4 * 2 + core, t)

    def at_t(k):
        return (dp, pipe, (t + k) % 4)

    other_core = (dp, y * 2 + 1 - core, t)

    loads = [
        pltpu.make_async_copy(
            ref.at[0], w.at[m, pl.ds(pl.multiple_of(dp * SHARD, SHARD), SHARD)], local.at[m]
        )
        for m, ref in enumerate((wq_hbm, wk_hbm, wv_hbm))
    ]
    enc_own = pltpu.make_async_copy(
        enc_hbm, enc64.at[pl.ds(pl.multiple_of(t * 16, 16), 16)], local.at[3]
    )
    x_load = pltpu.make_async_copy(x_hbm.at[0], xv, local.at[4])
    hg_load = pltpu.make_async_copy(hg_hbm.at[0], hg, local.at[5])
    og_load = pltpu.make_async_copy(
        og_hbm.at[0, :, pl.ds(pl.multiple_of(t * BLOCK, BLOCK), BLOCK)], og, local.at[6]
    )
    for copy in loads + [enc_own, x_load, hg_load, og_load]:
        copy.start()

    barrier = pltpu.get_barrier_semaphore()
    for k in range(1, 4):
        for peer in (at_z(k), at_x(k), at_y(k), at_t(k)):
            pl.semaphore_signal(barrier, inc=1, device_id=peer, device_id_type=MESH)
    pl.semaphore_signal(barrier, inc=1, device_id=other_core, device_id_type=MESH)
    for copy in loads + [enc_own]:
        copy.wait()
    pl.semaphore_wait(barrier, 13)

    def remote(src, dst, send, recv, peer):
        return pltpu.make_async_remote_copy(
            src_ref=src, dst_ref=dst, send_sem=send, recv_sem=recv,
            device_id=peer, device_id_type=MESH,
        )

    def piece(c, xx, zz, start=0, rows=CHUNK):
        first = (xx * 4 + zz) * SHARD + (c % SUBS) * CHUNK + start
        return w.at[c // SUBS, pl.ds(pl.multiple_of(first, HALF), rows)]

    def wait_bytes(sem, rows):
        part = w.at[0, pl.ds(0, rows)]
        pltpu.make_async_copy(part, part, sem).wait()

    def z_first(c):
        own = piece(c, x, z)
        for k in (1, -1):
            remote(own, own, z_send.at[c], z_near.at[c], at_z(k)).start()

    def z_second(c):
        up = piece(c, x, (z + 3) % 4, HALF, HALF)
        remote(up, up, z_send.at[c], z_far.at[c], at_z(1)).start()
        down = piece(c, x, (z + 1) % 4, 0, HALF)
        remote(down, down, z_send.at[c], z_far.at[c], at_z(-1)).start()

    def x_first(c, j):
        own = piece(c, x, (z + j) % 4)
        for k in (1, -1):
            remote(own, own, x_send.at[c], x_near.at[j, c], at_x(k)).start()

    def x_second(c, j):
        up = piece(c, (x + 3) % 4, (z + j) % 4, HALF, HALF)
        remote(up, up, x_send.at[c], x_far.at[j, c], at_x(1)).start()
        down = piece(c, (x + 1) % 4, (z + j) % 4, 0, HALF)
        remote(down, down, x_send.at[c], x_far.at[j, c], at_x(-1)).start()

    for c in range(Z_AHEAD):
        z_first(c)
    for c in range(X_AHEAD):
        x_first(c, 0)

    def enc_rows(p):
        return enc.at[pl.ds(pl.multiple_of(p * 16, 16), 16)]

    own16 = enc64.at[pl.ds(pl.multiple_of(t * 16, 16), 16)]
    for k in range(1, 4):
        remote(own16, own16, e_send.at[0], e_recv.at[0], at_t(k)).start()

    def enc_y():
        rows48 = enc64.at[pl.ds(0, 48)]
        pltpu.make_async_copy(rows48, rows48, e_recv.at[0]).wait()
        moved = regroup(enc64[...]).astype(jnp.bfloat16)
        for b in range(4):
            enc[pl.ds(pl.multiple_of(pipe * 16, 16), 16), b * BLOCK : (b + 1) * BLOCK] = moved[
                b * 16 : (b + 1) * 16
            ]
        mine = enc_rows(pipe)
        for k in range(1, 4):
            remote(mine, mine, e_send.at[1], e_recv.at[1], at_y(k)).start()

    def enc_core():
        rows48 = enc.at[pl.ds(0, 48)]
        pltpu.make_async_copy(rows48, rows48, e_recv.at[1]).wait()
        for k in range(4):
            mine = enc_rows(k * 2 + core)
            remote(mine, mine, e_send.at[2], e_recv.at[2], other_core).start()

    def enc_wait():
        rows64 = enc.at[pl.ds(0, 64)]
        pltpu.make_async_copy(rows64, rows64, e_recv.at[2]).wait()

    def norm():
        x_load.wait()
        total = jnp.zeros((ROWS, 1), jnp.float32)
        for b in range(4):
            part = xv[:, b * BLOCK : (b + 1) * BLOCK].astype(jnp.float32)
            total += jnp.sum(part * part, axis=1, keepdims=True)
        scale = lax.rsqrt(total / D + EPSILON)
        inv[...] = jnp.broadcast_to(scale, (ROWS, 128))
        for b in range(4):
            cols = slice(b * BLOCK, (b + 1) * BLOCK)
            normed = xv[:, cols].astype(jnp.float32) * scale
            hid[:, cols] = (normed * gain_ref[:, cols]).astype(jnp.bfloat16)

    def project(left, m, out):
        acc[...] = jnp.zeros_like(acc)

        @pl.loop(0, D // COLS)
        def _(k):
            at = pl.ds(pl.multiple_of(k * COLS, COLS), COLS)
            acc[...] += jnp.dot(left[:, at], w[m, at, :], preferred_element_type=jnp.float32)

        out[...] = acc[...].astype(jnp.bfloat16)

    steps = CHUNKS + 3

    @pl.loop(0, steps)
    def _(c):
        @pl.when(c < CHUNKS)
        def _():
            wait_bytes(z_near.at[c], 2 * CHUNK)
            z_second(c)

            @pl.when(c + Z_AHEAD < CHUNKS)
            def _():
                z_first(c + Z_AHEAD)

            x_first(c, 1)
            x_first(c, 3)
            wait_bytes(x_near.at[0, c], 2 * CHUNK)
            x_second(c, 0)

            @pl.when(c + X_AHEAD < CHUNKS)
            def _():
                x_first(c + X_AHEAD, 0)

        @pl.when(jnp.logical_and(c >= 1, c < CHUNKS + 1))
        def _():
            b = c - 1
            wait_bytes(z_far.at[b], CHUNK)
            x_first(b, 2)
            for j in (1, 3):
                wait_bytes(x_near.at[j, b], 2 * CHUNK)
                x_second(b, j)

        @pl.when(jnp.logical_and(c >= 2, c < CHUNKS + 2))
        def _():
            b = c - 2
            wait_bytes(x_near.at[2, b], 2 * CHUNK)
            x_second(b, 2)

        @pl.when(c >= 3)
        def _():
            b = c - 3
            for j in range(4):
                wait_bytes(x_far.at[j, b], CHUNK)

        pl.when(c == 0)(enc_y)
        pl.when(c == 1)(enc_core)
        pl.when(c == 2)(norm)

        @pl.when(c == SUBS + 2)
        def _():
            enc_wait()
            project(hid, 0, qb)

        @pl.when(c == 2 * SUBS + 2)
        def _():
            project(enc, 1, kb)

    project(enc, 2, vb)
    hg_load.wait()

    scale = 1.0 / math.sqrt(HEAD_DIM)
    for h in range(HEADS_HERE):
        cols = slice(h * HEAD_DIM, (h + 1) * HEAD_DIM)
        q, k, v, a = qb[:, cols], kb[:, cols], vb[:, cols], hg[:, cols]
        expo = jnp.exp(dot_nt(q, k) * scale)
        probs = expo / jnp.sum(expo, axis=1, keepdims=True)
        prob_grad = dot_nt(a, v)
        mean = jnp.sum(prob_grad * probs, axis=1, keepdims=True)
        score_grad = (probs * (prob_grad - mean) * scale).astype(jnp.bfloat16)
        dq[:, cols] = jnp.dot(score_grad, k, preferred_element_type=jnp.float32).astype(jnp.bfloat16)
        dk[:, cols] = dot_tn(score_grad, q).astype(jnp.bfloat16)
        dv[:, cols] = dot_tn(probs.astype(jnp.bfloat16), a).astype(jnp.bfloat16)

    inner[0] = jnp.zeros((ROWS, 128), jnp.float32)

    def hidden_block(j):
        at = pl.ds(pl.multiple_of(j * BLOCK, BLOCK), BLOCK)
        part = dot_nt(dq[...], w[0, at, :]).astype(jnp.bfloat16)
        hp[j] = part
        normed = xv[:, at].astype(jnp.float32) * inv[:, :1]
        product = part.astype(jnp.float32) * gain_ref[:, at] * normed
        folded = product[:, :128]
        for b in range(1, BLOCK // 128):
            folded += product[:, b * 128 : (b + 1) * 128]
        inner[0] += folded

    @pl.loop(1, 4)
    def _(k):
        j = (t + k) % 4
        hidden_block(j)
        remote(hp.at[j], hp_in.at[t], h_send.at[0], h_recv.at[0], at_t(k)).start()

    hidden_block(t)
    row = jnp.sum(inner[0].T, axis=0, keepdims=True)
    inner[1, pl.ds(0, 8)] = jnp.broadcast_to(row, (8, 128))
    for k in range(1, 4):
        remote(
            inner.at[1, pl.ds(0, 8)], inner.at[2, pl.ds(pl.multiple_of(t * 8, 8), 8)],
            i_send.at[0], i_recv.at[0], at_t(k),
        ).start()

    @pl.loop(0, D // COLS)
    def _(b):
        at = pl.ds(pl.multiple_of(b * COLS, COLS), COLS)
        de[:, at] = dot_nt(dk[...], w[1, at, :]) + dot_nt(dv[...], w[2, at, :])

    def pair_rows(k, c):
        return pl.ds(pl.multiple_of((k * 2 + c) * 16, 16), 16)

    for k in range(4):
        de1[k] = de[pair_rows(k, 1 - core), :].astype(jnp.bfloat16)
    remote(de1, de1_in, d_send.at[0], d_recv.at[0], other_core).start()
    pltpu.make_async_copy(de1_in, de1_in, d_recv.at[0]).wait()

    for k in range(1, 4):
        to = (y + k) % 4
        de2[to] = (de[pair_rows(to, core), :] + de1_in[to].astype(jnp.float32)).astype(jnp.bfloat16)
        remote(de2.at[to], de2_in.at[y], d_send.at[1], d_recv.at[1], at_y(k)).start()
    total = de[pair_rows(y, core), :] + de1_in[y].astype(jnp.float32)
    three = de2_in.at[pl.ds(0, 3)]
    pltpu.make_async_copy(three, three, d_recv.at[1]).wait()
    for k in range(1, 4):
        total += de2_in[(y + k) % 4].astype(jnp.float32)
    low = total.astype(jnp.bfloat16)
    stacked = jnp.concatenate([low[:, b * BLOCK : (b + 1) * BLOCK] for b in range(4)], axis=0)
    moved = regroup(stacked).astype(jnp.bfloat16)
    for b in range(4):
        de3[b] = moved[b * 16 : (b + 1) * 16]
    for k in range(1, 4):
        remote(
            de3.at[(t + k) % 4], de3_in.at[t], d_send.at[2], d_recv.at[2], at_t(k)
        ).start()

    og_load.wait()
    rows24 = inner.at[2, pl.ds(0, 24)]
    pltpu.make_async_copy(rows24, rows24, i_recv.at[0]).wait()
    row_total = row
    for k in range(1, 4):
        row_total += inner[2, pl.ds(pl.multiple_of((t + k) % 4 * 8, 8), 1)]
    mean = jnp.broadcast_to(row_total / D, (128, 128)).T[:, :1]
    three = hp_in.at[pl.ds(0, 3)]
    pltpu.make_async_copy(three, three, h_recv.at[0]).wait()
    hidden_grad = hp[t].astype(jnp.float32)
    for k in range(1, 4):
        hidden_grad += hp_in[(t + k) % 4].astype(jnp.float32)
    at = pl.ds(pl.multiple_of(t * BLOCK, BLOCK), BLOCK)
    scale_col = inv[:, :1]
    normed = xv[:, at].astype(jnp.float32) * scale_col
    own_gain = jnp.sum(hidden_grad * normed, axis=0, keepdims=True)
    gz[z] = own_gain
    for k in range(1, 4):
        remote(gz.at[z], gz.at[z], g_send.at[0], g_recv.at[0], at_z(k)).start()
    normed_grad = hidden_grad * gain_ref[:, at]
    ig_ref[0] = (
        og[...].astype(jnp.float32) + scale_col * (normed_grad - normed * mean)
    ).astype(jnp.bfloat16)

    three = gz.at[pl.ds(0, 3)]
    pltpu.make_async_copy(three, three, g_recv.at[0]).wait()
    gx[x] = gz[0] + gz[1] + gz[2] + gz[3]
    for k in range(1, 4):
        remote(gx.at[x], gx.at[x], g_send.at[1], g_recv.at[1], at_x(k)).start()

    three = de3_in.at[pl.ds(0, 3)]
    pltpu.make_async_copy(three, three, d_recv.at[2]).wait()
    summed = de3[t].astype(jnp.float32)
    for k in range(1, 4):
        summed += de3_in[(t + k) % 4].astype(jnp.float32)
    eg_ref[...] = summed

    three = gx.at[pl.ds(0, 3)]
    pltpu.make_async_copy(three, three, g_recv.at[1]).wait()
    gg_ref[...] = gx[0] + gx[1] + gx[2] + gx[3]

    @pl.loop(0, CHUNKS)
    def _(c):
        wait_bytes(z_send.at[c], 3 * CHUNK)
        wait_bytes(x_send.at[c], 12 * CHUNK)

    def sent(ref, sem):
        pltpu.make_async_copy(ref, ref, sem).wait()

    sent(enc64.at[pl.ds(0, 48)], e_send.at[0])
    sent(enc.at[pl.ds(0, 48)], e_send.at[1])
    sent(enc.at[pl.ds(0, 64)], e_send.at[2])
    sent(hp.at[pl.ds(0, 3)], h_send.at[0])
    sent(inner.at[2, pl.ds(0, 24)], i_send.at[0])
    sent(de1, d_send.at[0])
    sent(de2.at[pl.ds(0, 3)], d_send.at[1])
    sent(de3.at[pl.ds(0, 3)], d_send.at[2])
    sent(gz.at[pl.ds(0, 3)], g_send.at[0])
    sent(gx.at[pl.ds(0, 3)], g_send.at[1])


def shards(
    section_input, out_grad, head_grad, encoder, norm_gain, query_weight, key_weight, value_weight
):
    low, f32 = jnp.bfloat16, jnp.float32
    enc16 = encoder.reshape(4, 4, BLOCK).transpose(1, 0, 2).reshape(16, BLOCK)
    hbm = pl.BlockSpec(memory_space=pl.ANY)
    vmem = pl.BlockSpec(memory_space=pltpu.VMEM)
    dma = pltpu.SemaphoreType.DMA
    grads = pl.pallas_call(
        kernel,
        out_shape=(
            jax.ShapeDtypeStruct((1, ROWS, BLOCK), low),
            jax.ShapeDtypeStruct((16, BLOCK), f32),
            jax.ShapeDtypeStruct((1, BLOCK), f32),
        ),
        in_specs=[hbm, hbm, hbm, hbm, vmem, hbm, hbm, hbm],
        out_specs=(vmem, vmem, vmem),
        scratch_shapes=[
            pltpu.VMEM((3, D, COLS), low),
            pltpu.VMEM((ROWS, D), low),
            pltpu.VMEM((ROWS, BLOCK), low),
            pltpu.VMEM((ROWS, COLS), low),
            pltpu.VMEM((64, BLOCK), low),
            pltpu.VMEM((ROWS, D), low),
            pltpu.VMEM((ROWS, D), low),
            pltpu.VMEM((ROWS, 128), f32),
            pltpu.VMEM((ROWS, COLS), f32),
        ]
        + [pltpu.VMEM((ROWS, COLS), low)] * 6
        + [
            pltpu.VMEM((4, ROWS, BLOCK), low),
            pltpu.VMEM((4, ROWS, BLOCK), low),
            pltpu.VMEM((3, ROWS, 128), f32),
            pltpu.VMEM((ROWS, D), f32),
            pltpu.VMEM((4, 16, D), low),
            pltpu.VMEM((4, 16, D), low),
            pltpu.VMEM((4, 16, D), low),
            pltpu.VMEM((4, 16, D), low),
            pltpu.VMEM((4, 16, BLOCK), low),
            pltpu.VMEM((4, 16, BLOCK), low),
            pltpu.VMEM((4, 1, BLOCK), f32),
            pltpu.VMEM((4, 1, BLOCK), f32),
            dma((7,)),
            dma((CHUNKS,)),
            dma((CHUNKS,)),
            dma((CHUNKS,)),
            dma((CHUNKS,)),
            dma((4, CHUNKS)),
            dma((4, CHUNKS)),
            dma((3,)),
            dma((3,)),
            dma((1,)),
            dma((1,)),
            dma((1,)),
            dma((1,)),
            dma((3,)),
            dma((3,)),
            dma((2,)),
            dma((2,)),
        ],
        compiler_params=pltpu.CompilerParams(
            collective_id=0, has_side_effects=True, vmem_limit_bytes=48 * 1024 * 1024
        ),
        cost_estimate=pl.CostEstimate(
            flops=6 * 2 * ROWS * D * COLS, bytes_accessed=4 * 1024 * 1024, transcendentals=0
        ),
    )(
        section_input, out_grad, head_grad, enc16, norm_gain,
        query_weight, key_weight, value_weight,
    )
    input_grad, enc_grad, gain_grad = grads
    enc_grad = enc_grad.reshape(4, 4, BLOCK).transpose(1, 0, 2).reshape(4, D)
    return input_grad, enc_grad, gain_grad


def solution(mesh):
    placed = (
        P("pipe", "dp", None),
        P("pipe", "dp", None),
        P("pipe", "dp", "tensor"),
        P(("dp", "pipe", "tensor"), None),
        P("pipe", None),
        P("pipe", "dp", "tensor"),
        P("pipe", "dp", "tensor"),
        P("pipe", "dp", "tensor"),
    )
    return jax.shard_map(
        shards,
        mesh=mesh,
        in_specs=placed,
        out_specs=(
            P("pipe", "dp", "tensor"),
            P(("dp", "pipe", "tensor"), None),
            P("pipe", "tensor"),
        ),
        check_vma=False,
    )
```

```python
import functools
import math

import jax
import jax.numpy as jnp
from jax import lax
from jax.experimental import pallas as pl
from jax.experimental.pallas import tpu as pltpu
from jax.sharding import PartitionSpec as P

HEAD_DIM = 256
HEADS_HERE = 2
COLS = 512
D = 4096
ROWS = 128
SHARD = 256
BLOCK = 1024
EPSILON = 1e-06

SUBS = 4
CHUNK = SHARD // SUBS
HALF = CHUNK // 2
CHUNKS = 3 * SUBS
Z_AHEAD = 2
X_AHEAD = 12
MESH = pl.DeviceIdType.MESH


def dot_nt(left, right):
    return lax.dot_general(
        left, right, (((1,), (1,)), ((), ())), preferred_element_type=jnp.float32
    )


def dot_tn(left, right):
    return lax.dot_general(
        left, right, (((0,), (0,)), ((), ())), preferred_element_type=jnp.float32
    )


def regroup(rows):
    i = lax.broadcasted_iota(jnp.int32, (64, 64), 0)
    j = lax.broadcasted_iota(jnp.int32, (64, 64), 1)
    source = (i % 16) // 4 * 16 + i // 16 * 4 + i % 4
    hot = jnp.where(j == source, 1.0, 0.0).astype(jnp.bfloat16)
    return jnp.dot(hot, rows, preferred_element_type=jnp.float32)


def kernel(
    x_hbm, og_hbm, hg_hbm, enc_hbm, gain_ref, wq_hbm, wk_hbm, wv_hbm,
    ig_ref, eg_ref, gg_ref,
    w, xv, og, hg, enc64, enc, hid, inv, acc, qb, kb, vb, dq, dk, dv,
    hp, hp_in, note, note_in, de, de1, de1_in, de2, de2_in, de3, de3_in, gz, gx,
    local, z_send, x_send, z_near, z_far, x_near, x_far,
    e_send, e_recv, h_send, h_recv, i_send, i_recv, d_send, d_recv, g_send, g_recv,
):
    dp = lax.axis_index("dp")
    pipe = lax.axis_index("pipe")
    t = lax.axis_index("tensor")
    x, z = dp // 4, dp % 4
    y, core = pipe // 2, pipe % 2

    def at_z(k):
        return (x * 4 + (z + k) % 4, pipe, t)

    def at_x(k):
        return ((x + k) % 4 * 4 + z, pipe, t)

    def at_y(k):
        return (dp, (y + k) % 4 * 2 + core, t)

    def at_t(k):
        return (dp, pipe, (t + k) % 4)

    other_core = (dp, y * 2 + 1 - core, t)

    loads = [
        pltpu.make_async_copy(
            ref.at[0], w.at[m, pl.ds(pl.multiple_of(dp * SHARD, SHARD), SHARD)], local.at[m]
        )
        for m, ref in enumerate((wq_hbm, wk_hbm, wv_hbm))
    ]
    enc_own = pltpu.make_async_copy(
        enc_hbm, enc64.at[pl.ds(pl.multiple_of(t * 16, 16), 16)], local.at[3]
    )
    x_load = pltpu.make_async_copy(x_hbm.at[0], xv, local.at[4])
    hg_load = pltpu.make_async_copy(hg_hbm.at[0], hg, local.at[5])
    og_load = pltpu.make_async_copy(
        og_hbm.at[0, :, pl.ds(pl.multiple_of(t * BLOCK, BLOCK), BLOCK)], og, local.at[6]
    )
    for copy in loads + [enc_own, x_load, hg_load, og_load]:
        copy.start()

    barrier = pltpu.get_barrier_semaphore()
    for k in range(1, 4):
        for peer in (at_z(k), at_x(k), at_y(k), at_t(k)):
            pl.semaphore_signal(barrier, inc=1, device_id=peer, device_id_type=MESH)
    pl.semaphore_signal(barrier, inc=1, device_id=other_core, device_id_type=MESH)
    for copy in loads + [enc_own]:
        copy.wait()
    pl.semaphore_wait(barrier, 13)

    def remote(src, dst, send, recv, peer):
        return pltpu.make_async_remote_copy(
            src_ref=src, dst_ref=dst, send_sem=send, recv_sem=recv,
            device_id=peer, device_id_type=MESH,
        )

    def piece(c, xx, zz, start=0, rows=CHUNK):
        first = (xx * 4 + zz) * SHARD + (c % SUBS) * CHUNK + start
        return w.at[c // SUBS, pl.ds(pl.multiple_of(first, HALF), rows)]

    def wait_bytes(sem, rows):
        part = w.at[0, pl.ds(0, rows)]
        pltpu.make_async_copy(part, part, sem).wait()

    def z_first(c):
        own = piece(c, x, z)
        for k in (1, -1):
            remote(own, own, z_send.at[c], z_near.at[c], at_z(k)).start()

    def z_second(c):
        up = piece(c, x, (z + 3) % 4, HALF, HALF)
        remote(up, up, z_send.at[c], z_far.at[c], at_z(1)).start()
        down = piece(c, x, (z + 1) % 4, 0, HALF)
        remote(down, down, z_send.at[c], z_far.at[c], at_z(-1)).start()

    def x_first(c, j):
        own = piece(c, x, (z + j) % 4)
        for k in (1, -1):
            remote(own, own, x_send.at[c], x_near.at[j, c], at_x(k)).start()

    def x_second(c, j):
        up = piece(c, (x + 3) % 4, (z + j) % 4, HALF, HALF)
        remote(up, up, x_send.at[c], x_far.at[j, c], at_x(1)).start()
        down = piece(c, (x + 1) % 4, (z + j) % 4, 0, HALF)
        remote(down, down, x_send.at[c], x_far.at[j, c], at_x(-1)).start()

    for c in range(Z_AHEAD):
        z_first(c)
    for c in range(X_AHEAD):
        x_first(c, 0)

    def enc_rows(p):
        return enc.at[pl.ds(pl.multiple_of(p * 16, 16), 16)]

    own16 = enc64.at[pl.ds(pl.multiple_of(t * 16, 16), 16)]
    for k in range(1, 4):
        remote(own16, own16, e_send.at[0], e_recv.at[0], at_t(k)).start()

    def enc_y():
        rows48 = enc64.at[pl.ds(0, 48)]
        pltpu.make_async_copy(rows48, rows48, e_recv.at[0]).wait()
        moved = regroup(enc64[...]).astype(jnp.bfloat16)
        for b in range(4):
            enc[pl.ds(pl.multiple_of(pipe * 16, 16), 16), b * BLOCK : (b + 1) * BLOCK] = moved[
                b * 16 : (b + 1) * 16
            ]
        mine = enc_rows(pipe)
        for k in range(1, 4):
            remote(mine, mine, e_send.at[1], e_recv.at[1], at_y(k)).start()

    def enc_core():
        rows48 = enc.at[pl.ds(0, 48)]
        pltpu.make_async_copy(rows48, rows48, e_recv.at[1]).wait()
        for k in range(4):
            mine = enc_rows(k * 2 + core)
            remote(mine, mine, e_send.at[2], e_recv.at[2], other_core).start()

    def enc_wait():
        rows64 = enc.at[pl.ds(0, 64)]
        pltpu.make_async_copy(rows64, rows64, e_recv.at[2]).wait()

    def norm():
        x_load.wait()
        total = jnp.zeros((ROWS, 1), jnp.float32)
        for b in range(4):
            part = xv[:, b * BLOCK : (b + 1) * BLOCK].astype(jnp.float32)
            total += jnp.sum(part * part, axis=1, keepdims=True)
        scale = lax.rsqrt(total / D + EPSILON)
        inv[...] = jnp.broadcast_to(scale, (ROWS, 128))
        for b in range(4):
            cols = slice(b * BLOCK, (b + 1) * BLOCK)
            normed = xv[:, cols].astype(jnp.float32) * scale
            hid[:, cols] = (normed * gain_ref[:, cols]).astype(jnp.bfloat16)

    def project(left, m, out):
        acc[...] = jnp.zeros_like(acc)

        @pl.loop(0, D // COLS)
        def _(k):
            at = pl.ds(pl.multiple_of(k * COLS, COLS), COLS)
            acc[...] += jnp.dot(left[:, at], w[m, at, :], preferred_element_type=jnp.float32)

        out[...] = acc[...].astype(jnp.bfloat16)

    steps = CHUNKS + 3

    @pl.loop(0, steps)
    def _(c):
        @pl.when(c < CHUNKS)
        def _():
            wait_bytes(z_near.at[c], 2 * CHUNK)
            z_second(c)

            @pl.when(c + Z_AHEAD < CHUNKS)
            def _():
                z_first(c + Z_AHEAD)

            x_first(c, 1)
            x_first(c, 3)
            wait_bytes(x_near.at[0, c], 2 * CHUNK)
            x_second(c, 0)

            @pl.when(c + X_AHEAD < CHUNKS)
            def _():
                x_first(c + X_AHEAD, 0)

        @pl.when(jnp.logical_and(c >= 1, c < CHUNKS + 1))
        def _():
            b = c - 1
            wait_bytes(z_far.at[b], CHUNK)
            x_first(b, 2)
            for j in (1, 3):
                wait_bytes(x_near.at[j, b], 2 * CHUNK)
                x_second(b, j)

        @pl.when(jnp.logical_and(c >= 2, c < CHUNKS + 2))
        def _():
            b = c - 2
            wait_bytes(x_near.at[2, b], 2 * CHUNK)
            x_second(b, 2)

        @pl.when(c >= 3)
        def _():
            b = c - 3
            for j in range(4):
                wait_bytes(x_far.at[j, b], CHUNK)

        pl.when(c == 0)(enc_y)
        pl.when(c == 1)(enc_core)
        pl.when(c == 2)(norm)

        @pl.when(c == SUBS + 2)
        def _():
            enc_wait()
            project(hid, 0, qb)

        @pl.when(c == 2 * SUBS + 2)
        def _():
            project(enc, 1, kb)

    project(enc, 2, vb)
    hg_load.wait()

    scale = 1.0 / math.sqrt(HEAD_DIM)
    for h in range(HEADS_HERE):
        cols = slice(h * HEAD_DIM, (h + 1) * HEAD_DIM)
        q, k, v, a = qb[:, cols], kb[:, cols], vb[:, cols], hg[:, cols]
        expo = jnp.exp(dot_nt(q, k) * scale)
        probs = expo / jnp.sum(expo, axis=1, keepdims=True)
        prob_grad = dot_nt(a, v)
        mean = jnp.sum(prob_grad * probs, axis=1, keepdims=True)
        score_grad = (probs * (prob_grad - mean) * scale).astype(jnp.bfloat16)
        dq[:, cols] = jnp.dot(score_grad, k, preferred_element_type=jnp.float32).astype(jnp.bfloat16)
        dk[:, cols] = dot_tn(score_grad, q).astype(jnp.bfloat16)
        dv[:, cols] = dot_tn(probs.astype(jnp.bfloat16), a).astype(jnp.bfloat16)

    note[...] = jnp.zeros_like(note)

    def hidden_block(j):
        at = pl.ds(pl.multiple_of(j * BLOCK, BLOCK), BLOCK)
        part = dot_nt(dq[...], w[0, at, :]).astype(jnp.bfloat16)
        hp[j] = part
        product = part.astype(jnp.float32) * (xv[:, at].astype(jnp.float32) * inv[:, :1])
        gain = jnp.sum(product, axis=0, keepdims=True)
        product *= gain_ref[:, at]
        folded = product[:, :128]
        for b in range(8):
            note[j, pl.ds(8 + b, 1)] = gain[:, b * 128 : (b + 1) * 128]
            if b:
                folded += product[:, b * 128 : (b + 1) * 128]
        return folded

    def hidden_step(k, folded):
        j = (t + k) % 4
        folded += hidden_block(j)
        remote(hp.at[j], hp_in.at[t], h_send.at[0], h_recv.at[0], at_t(k)).start()
        return folded

    folded = lax.fori_loop(1, 4, hidden_step, jnp.zeros((ROWS, 128), jnp.float32))
    folded += hidden_block(t)
    row = jnp.sum(folded.T, axis=0, keepdims=True)
    for j in range(4):
        note[j, pl.ds(0, 1)] = row
    for k in range(1, 4):
        remote(
            note.at[(t + k) % 4], note_in.at[t], i_send.at[0], i_recv.at[0], at_t(k)
        ).start()

    @pl.loop(0, D // COLS)
    def _(b):
        at = pl.ds(pl.multiple_of(b * COLS, COLS), COLS)
        de[:, at] = dot_nt(dk[...], w[1, at, :]) + dot_nt(dv[...], w[2, at, :])

    def pair_rows(k, c):
        return pl.ds(pl.multiple_of((k * 2 + c) * 16, 16), 16)

    def arrived(ref, sem):
        three = ref.at[pl.ds(0, 3)]
        pltpu.make_async_copy(three, three, sem).wait()

    for k in range(4):
        de1[k] = de[pair_rows(k, 1 - core), :].astype(jnp.bfloat16)
    remote(de1, de1_in, d_send.at[0], d_recv.at[0], other_core).start()

    arrived(note_in, i_recv.at[0])
    note_in[t] = note[t]
    noted = note_in[0] + note_in[1] + note_in[2] + note_in[3]
    gz[z] = noted[8:]
    for k in range(1, 4):
        remote(gz.at[z], gz.at[z], g_send.at[0], g_recv.at[0], at_z(k)).start()
    mean = jnp.broadcast_to(noted[:1] / D, (128, 128)).T[:, :1]

    pltpu.make_async_copy(de1_in, de1_in, d_recv.at[0]).wait()
    for k in range(1, 4):
        to = (y + k) % 4
        de2[to] = (de[pair_rows(to, core), :] + de1_in[to].astype(jnp.float32)).astype(jnp.bfloat16)
        remote(de2.at[to], de2_in.at[y], d_send.at[1], d_recv.at[1], at_y(k)).start()
    total = de[pair_rows(y, core), :] + de1_in[y].astype(jnp.float32)

    arrived(gz, g_recv.at[0])
    gx[x] = gz[0] + gz[1] + gz[2] + gz[3]
    for k in range(1, 4):
        remote(gx.at[x], gx.at[x], g_send.at[1], g_recv.at[1], at_x(k)).start()

    arrived(de2_in, d_recv.at[1])
    for k in range(1, 4):
        total += de2_in[(y + k) % 4].astype(jnp.float32)
    low = total.astype(jnp.bfloat16)
    stacked = jnp.concatenate([low[:, b * BLOCK : (b + 1) * BLOCK] for b in range(4)], axis=0)
    moved = regroup(stacked).astype(jnp.bfloat16)
    for b in range(4):
        de3[b] = moved[b * 16 : (b + 1) * 16]
    for k in range(1, 4):
        remote(
            de3.at[(t + k) % 4], de3_in.at[t], d_send.at[2], d_recv.at[2], at_t(k)
        ).start()
    arrived(gx, g_recv.at[1])
    gains = gx[0] + gx[1] + gx[2] + gx[3]
    for b in range(8):
        gg_ref[:, b * 128 : (b + 1) * 128] = gains[b : b + 1]

    og_load.wait()
    at = pl.ds(pl.multiple_of(t * BLOCK, BLOCK), BLOCK)
    scale_col = inv[:, :1]
    normed = xv[:, at].astype(jnp.float32) * scale_col
    arrived(hp_in, h_recv.at[0])
    hidden_grad = hp[t].astype(jnp.float32)
    for k in range(1, 4):
        hidden_grad += hp_in[(t + k) % 4].astype(jnp.float32)
    normed_grad = hidden_grad * gain_ref[:, at]
    ig_ref[0] = (
        og[...].astype(jnp.float32) + scale_col * (normed_grad - normed * mean)
    ).astype(jnp.bfloat16)

    arrived(de3_in, d_recv.at[2])
    summed = de3[t].astype(jnp.float32)
    for k in range(1, 4):
        summed += de3_in[(t + k) % 4].astype(jnp.float32)
    eg_ref[...] = summed

    @pl.loop(0, CHUNKS)
    def _(c):
        wait_bytes(z_send.at[c], 3 * CHUNK)
        wait_bytes(x_send.at[c], 12 * CHUNK)

    def sent(ref, sem):
        pltpu.make_async_copy(ref, ref, sem).wait()

    sent(enc64.at[pl.ds(0, 48)], e_send.at[0])
    sent(enc.at[pl.ds(0, 48)], e_send.at[1])
    sent(enc.at[pl.ds(0, 64)], e_send.at[2])
    sent(hp.at[pl.ds(0, 3)], h_send.at[0])
    sent(note.at[pl.ds(0, 3)], i_send.at[0])
    sent(de1, d_send.at[0])
    sent(de2.at[pl.ds(0, 3)], d_send.at[1])
    sent(de3.at[pl.ds(0, 3)], d_send.at[2])
    sent(gz.at[pl.ds(0, 3)], g_send.at[0])
    sent(gx.at[pl.ds(0, 3)], g_send.at[1])


def shards(
    section_input, out_grad, head_grad, encoder, norm_gain, query_weight, key_weight, value_weight
):
    low, f32 = jnp.bfloat16, jnp.float32
    enc16 = encoder.reshape(4, 4, BLOCK).transpose(1, 0, 2).reshape(16, BLOCK)
    hbm = pl.BlockSpec(memory_space=pl.ANY)
    vmem = pl.BlockSpec(memory_space=pltpu.VMEM)
    dma = pltpu.SemaphoreType.DMA
    grads = pl.pallas_call(
        kernel,
        out_shape=(
            jax.ShapeDtypeStruct((1, ROWS, BLOCK), low),
            jax.ShapeDtypeStruct((16, BLOCK), f32),
            jax.ShapeDtypeStruct((1, BLOCK), f32),
        ),
        in_specs=[hbm, hbm, hbm, hbm, vmem, hbm, hbm, hbm],
        out_specs=(vmem, vmem, vmem),
        scratch_shapes=[
            pltpu.VMEM((3, D, COLS), low),
            pltpu.VMEM((ROWS, D), low),
            pltpu.VMEM((ROWS, BLOCK), low),
            pltpu.VMEM((ROWS, COLS), low),
            pltpu.VMEM((64, BLOCK), low),
            pltpu.VMEM((ROWS, D), low),
            pltpu.VMEM((ROWS, D), low),
            pltpu.VMEM((ROWS, 128), f32),
            pltpu.VMEM((ROWS, COLS), f32),
        ]
        + [pltpu.VMEM((ROWS, COLS), low)] * 6
        + [
            pltpu.VMEM((4, ROWS, BLOCK), low),
            pltpu.VMEM((4, ROWS, BLOCK), low),
            pltpu.VMEM((4, 16, 128), f32),
            pltpu.VMEM((4, 16, 128), f32),
            pltpu.VMEM((ROWS, D), f32),
            pltpu.VMEM((4, 16, D), low),
            pltpu.VMEM((4, 16, D), low),
            pltpu.VMEM((4, 16, D), low),
            pltpu.VMEM((4, 16, D), low),
            pltpu.VMEM((4, 16, BLOCK), low),
            pltpu.VMEM((4, 16, BLOCK), low),
            pltpu.VMEM((4, 8, 128), f32),
            pltpu.VMEM((4, 8, 128), f32),
            dma((7,)),
            dma((CHUNKS,)),
            dma((CHUNKS,)),
            dma((CHUNKS,)),
            dma((CHUNKS,)),
            dma((4, CHUNKS)),
            dma((4, CHUNKS)),
            dma((3,)),
            dma((3,)),
            dma((1,)),
            dma((1,)),
            dma((1,)),
            dma((1,)),
            dma((3,)),
            dma((3,)),
            dma((2,)),
            dma((2,)),
        ],
        compiler_params=pltpu.CompilerParams(
            collective_id=0, has_side_effects=True, vmem_limit_bytes=60 * 1024 * 1024
        ),
        cost_estimate=pl.CostEstimate(
            flops=6 * 2 * ROWS * D * COLS, bytes_accessed=4 * 1024 * 1024, transcendentals=0
        ),
    )(
        section_input, out_grad, head_grad, enc16, norm_gain,
        query_weight, key_weight, value_weight,
    )
    input_grad, enc_grad, gain_grad = grads
    enc_grad = enc_grad.reshape(4, 4, BLOCK).transpose(1, 0, 2).reshape(4, D)
    return input_grad, enc_grad, gain_grad


def solution(mesh):
    placed = (
        P("pipe", "dp", None),
        P("pipe", "dp", None),
        P("pipe", "dp", "tensor"),
        P(("dp", "pipe", "tensor"), None),
        P("pipe", None),
        P("pipe", "dp", "tensor"),
        P("pipe", "dp", "tensor"),
        P("pipe", "dp", "tensor"),
    )
    return jax.shard_map(
        shards,
        mesh=mesh,
        in_specs=placed,
        out_specs=(
            P("pipe", "dp", "tensor"),
            P(("dp", "pipe", "tensor"), None),
            P("pipe", "tensor"),
        ),
        check_vma=False,
    )
```

```python
import math

import jax
import jax.numpy as jnp
from jax import lax
from jax.experimental import pallas as pl
from jax.experimental.pallas import tpu as pltpu
from jax.sharding import PartitionSpec as P

HEAD_DIM = 256
HEADS_HERE = 2
COLS = 512
D = 4096
ROWS = 128
SHARD = 256
HALF = SHARD // 2
BLOCK = 1024
EPSILON = 1e-06
MESH = pl.DeviceIdType.MESH


def dot_nt(left, right):
    return lax.dot_general(
        left, right, (((1,), (1,)), ((), ())), preferred_element_type=jnp.float32
    )


def dot_tn(left, right):
    return lax.dot_general(
        left, right, (((0,), (0,)), ((), ())), preferred_element_type=jnp.float32
    )


def regroup(rows):
    i = lax.broadcasted_iota(jnp.int32, (64, 64), 0)
    j = lax.broadcasted_iota(jnp.int32, (64, 64), 1)
    source = (i % 16) // 4 * 16 + i // 16 * 4 + i % 4
    hot = jnp.where(j == source, 1.0, 0.0).astype(jnp.bfloat16)
    return jnp.dot(hot, rows, preferred_element_type=jnp.float32)


def kernel(
    x_hbm, og_hbm, hg_hbm, enc_ref, gain_ref, wq_hbm, wk_hbm, wv_hbm,
    ig_ref, eg_ref, gg_ref,
    wq, wkv, xv, og, hg, lines, enc64, encx, enc, hid, inv, part, part_in, kv, qb, probs, dq, dkv,
    hp, hp_in, note, note_in, de, de1, de1_in, de2, de2_in, dex, dex_in, de3, de3_in, gz, gx,
    local, z_send, x_send, z_near, z_far, x_near, x_far, p_send, p_recv, k_send, k_recv,
    e_send, e_recv, h_send, h_recv, i_send, i_recv, d_send, d_recv, g_send, g_recv,
):
    dp = lax.axis_index("dp")
    pipe = lax.axis_index("pipe")
    t = lax.axis_index("tensor")
    x, z = dp // 4, dp % 4
    y, core = pipe // 2, pipe % 2

    def at_z(k):
        return (x * 4 + (z + k) % 4, pipe, t)

    def at_x(k):
        return ((x + k) % 4 * 4 + z, pipe, t)

    def at_y(k):
        return (dp, (y + k) % 4 * 2 + core, t)

    def at_t(k):
        return (dp, pipe, (t + k) % 4)

    other_core = (dp, y * 2 + 1 - core, t)

    def remote(src, dst, send, recv, peer):
        return pltpu.make_async_remote_copy(
            src_ref=src, dst_ref=dst, send_sem=send, recv_sem=recv,
            device_id=peer, device_id_type=MESH,
        )

    def rows_of(ref, block, rows, start=0):
        return ref.at[pl.ds(pl.multiple_of(block * rows + start, 16), rows)]

    def wait_for(ref, sem):
        pltpu.make_async_copy(ref, ref, sem).wait()

    def arrived(ref, sem):
        wait_for(ref.at[pl.ds(0, 3)], sem)

    def piece(c, xx, zz, start=0, rows=SHARD):
        m, h = c // 2, c % 2
        if m == 0:
            first = (xx * 4 + zz) * SHARD + start
            return wq.at[h, pl.ds(pl.multiple_of(first, HALF), rows)]
        return wkv.at[m - 1, h, pl.ds(pl.multiple_of(zz * SHARD + start, HALF), rows)]

    sources = (wq_hbm, wk_hbm, wv_hbm)
    loads = [
        pltpu.make_async_copy(
            sources[c // 2].at[0, :, pl.ds(c % 2 * HEAD_DIM, HEAD_DIM)], piece(c, x, z), local.at[c]
        )
        for c in range(6)
    ]
    x_load = pltpu.make_async_copy(x_hbm.at[0], xv, local.at[7])
    hg_load = pltpu.make_async_copy(hg_hbm.at[0], hg, local.at[8])
    og_load = pltpu.make_async_copy(
        og_hbm.at[0, :, pl.ds(pl.multiple_of(t * BLOCK, BLOCK), BLOCK)], og, local.at[9]
    )
    for copy in loads + [x_load, hg_load, og_load]:
        copy.start()

    barrier = pltpu.get_barrier_semaphore()
    for k in range(1, 4):
        for peer in (at_z(k), at_x(k), at_y(k), at_t(k)):
            pl.semaphore_signal(barrier, inc=1, device_id=peer, device_id_type=MESH)
    pl.semaphore_signal(barrier, inc=1, device_id=other_core, device_id_type=MESH)
    for b in range(4):
        lines[pl.ds(b * 4, 4), :] = enc_ref[:, b * BLOCK : (b + 1) * BLOCK].astype(jnp.float32)
    enc64[pl.ds(pl.multiple_of(t * 16, 16), 16), :] = lines[...].astype(jnp.bfloat16)
    for copy in loads:
        copy.wait()
    pl.semaphore_wait(barrier, 13)

    def wait_bytes(sem, rows):
        wait_for(wq.at[0, pl.ds(0, rows)], sem)

    def z_first(c):
        own = piece(c, x, z)
        for k in (1, -1):
            remote(own, own, z_send.at[c], z_near.at[c], at_z(k)).start()

    def z_second(c):
        wait_bytes(z_near.at[c], 2 * SHARD)
        up = piece(c, x, (z + 3) % 4, HALF, HALF)
        remote(up, up, z_send.at[c], z_far.at[c], at_z(1)).start()
        down = piece(c, x, (z + 1) % 4, 0, HALF)
        remote(down, down, z_send.at[c], z_far.at[c], at_z(-1)).start()

    def x_first(h, j):
        own = piece(h, x, (z + j) % 4)
        for k in (1, -1):
            remote(own, own, x_send.at[h], x_near.at[j, h], at_x(k)).start()

    def x_second(h, j):
        wait_bytes(x_near.at[j, h], 2 * SHARD)
        up = piece(h, (x + 3) % 4, (z + j) % 4, HALF, HALF)
        remote(up, up, x_send.at[h], x_far.at[j, h], at_x(1)).start()
        down = piece(h, (x + 1) % 4, (z + j) % 4, 0, HALF)
        remote(down, down, x_send.at[h], x_far.at[j, h], at_x(-1)).start()

    own16 = rows_of(enc64, t, 16)
    for k in range(1, 4):
        remote(own16, own16, e_send.at[0], e_recv.at[0], at_t(k)).start()
    z_first(0)
    z_first(1)
    x_first(0, 0)
    x_first(1, 0)

    def enc_x():
        wait_for(enc64.at[pl.ds(0, 48)], e_recv.at[0])
        moved = regroup(enc64[...]).astype(jnp.bfloat16)
        for b in range(4):
            encx[b] = moved[b * 16 : (b + 1) * 16]
        enc[pl.ds(pl.multiple_of(pipe * 64 + x * 16, 16), 16), :] = encx[x]
        for k in range(1, 4):
            remote(
                encx.at[(x + k) % 4],
                enc.at[pl.ds(pl.multiple_of(pipe * 64 + x * 16, 16), 16)],
                e_send.at[1], e_recv.at[1], at_x(k),
            ).start()

    def enc_y():
        wait_for(enc.at[pl.ds(0, 48)], e_recv.at[1])
        mine = rows_of(enc, pipe, 64)
        for k in range(1, 4):
            remote(mine, mine, e_send.at[2], e_recv.at[2], at_y(k)).start()

    def enc_core():
        wait_for(enc.at[pl.ds(0, 192)], e_recv.at[2])
        for k in range(4):
            mine = rows_of(enc, k * 2 + core, 64)
            remote(mine, mine, e_send.at[3], e_recv.at[3], other_core).start()

    def norm():
        x_load.wait()
        total = jnp.zeros((ROWS, 1), jnp.float32)
        for b in range(4):
            block = xv[:, b * BLOCK : (b + 1) * BLOCK].astype(jnp.float32)
            total += jnp.sum(block * block, axis=1, keepdims=True)
        scale = lax.rsqrt(total / D + EPSILON)
        inv[...] = jnp.broadcast_to(scale, (ROWS, 128))
        for b in range(4):
            cols = slice(b * BLOCK, (b + 1) * BLOCK)
            normed = xv[:, cols].astype(jnp.float32) * scale
            hid[:, cols] = (normed * gain_ref[:, cols]).astype(jnp.bfloat16)

    def share(m, h):
        wait_bytes(z_far.at[2 + 2 * m + h], SHARD)
        rows = jnp.dot(enc[...], wkv[m, h], preferred_element_type=jnp.float32).astype(jnp.bfloat16)
        for p in range(8):
            for b in range(4):
                part[m, h, b, pl.ds(p * 16, 16), :] = rows[p * 64 + b * 16 : p * 64 + (b + 1) * 16]
        for k in range(1, 4):
            remote(
                part.at[m, h, (x + k) % 4], part_in.at[m, h, x],
                p_send.at[m, h], p_recv.at[m, h], at_x(k),
            ).start()

    def combine(m, h):
        arrived(part_in.at[m, h], p_recv.at[m, h])
        total = part[m, h, x].astype(jnp.float32)
        for k in range(1, 4):
            total += part_in[m, h, (x + k) % 4].astype(jnp.float32)
        kv[m, h] = total.astype(jnp.bfloat16)

    scale = 1.0 / math.sqrt(HEAD_DIM)

    def spread(m, h, grad):
        dkv[m, h, x] = grad.astype(jnp.bfloat16)
        mine = dkv.at[m, h, x]
        for k in range(1, 4):
            remote(mine, mine, k_send.at[m, h], k_recv.at[m, h], at_x(k)).start()

    def queries(h):
        for j in range(4):
            wait_bytes(x_far.at[j, h], SHARD)
        total = jnp.zeros((ROWS, HEAD_DIM), jnp.float32)

        def add(k, total):
            at = pl.ds(pl.multiple_of(k * BLOCK, BLOCK), BLOCK)
            return total + jnp.dot(hid[:, at], wq[h, at, :], preferred_element_type=jnp.float32)

        qb[h] = lax.fori_loop(0, 4, add, total).astype(jnp.bfloat16)

    def soften(h):
        expo = jnp.exp(dot_nt(qb[h], kv[0, h]) * scale)
        soft = expo / jnp.sum(expo, axis=1, keepdims=True)
        probs[h] = soft
        head = hg[:, h * HEAD_DIM : (h + 1) * HEAD_DIM]
        spread(1, h, dot_tn(soft.astype(jnp.bfloat16), head))

    def attend(h):
        soft = probs[h]
        prob_grad = dot_nt(hg[:, h * HEAD_DIM : (h + 1) * HEAD_DIM], kv[1, h])
        mean = jnp.sum(prob_grad * soft, axis=1, keepdims=True)
        score_grad = (soft * (prob_grad - mean) * scale).astype(jnp.bfloat16)
        spread(0, h, dot_tn(score_grad, qb[h]))
        dq[h] = jnp.dot(score_grad, kv[0, h], preferred_element_type=jnp.float32).astype(
            jnp.bfloat16
        )

    def term(m, h, cols):
        left = dkv[m, h].reshape(4 * ROWS, HEAD_DIM)
        return dot_nt(left, wkv[m, h, cols, :])

    def early_encoder():
        arrived(dkv.at[1, 0], k_recv.at[1, 0])
        arrived(dkv.at[1, 1], k_recv.at[1, 1])

        @pl.loop(0, 4)
        def _(b):
            at = pl.ds(pl.multiple_of(b * HEAD_DIM, HEAD_DIM), HEAD_DIM)
            de[:, at] = term(1, 0, at)

    z_second(0)
    z_first(2)
    x_first(0, 1)
    x_first(0, 3)
    enc_x()
    norm()
    x_second(0, 0)
    x_second(1, 0)

    z_second(1)
    z_first(3)
    x_first(1, 1)
    x_first(1, 3)
    enc_y()
    wait_bytes(z_far.at[0], SHARD)
    x_first(0, 2)
    x_second(0, 1)
    x_second(0, 3)

    z_second(2)
    z_first(4)
    enc_core()
    wait_bytes(z_far.at[1], SHARD)
    x_first(1, 2)
    x_second(0, 2)
    x_second(1, 1)
    x_second(1, 3)

    z_second(3)
    z_first(5)
    x_second(1, 2)
    wait_for(enc.at[pl.ds(0, 256)], e_recv.at[3])
    share(0, 0)
    queries(0)
    queries(1)
    hg_load.wait()

    z_second(4)
    combine(0, 0)
    soften(0)

    z_second(5)
    share(0, 1)
    share(1, 0)
    combine(0, 1)
    soften(1)
    combine(1, 0)
    attend(0)

    share(1, 1)
    early_encoder()
    combine(1, 1)
    attend(1)

    note[...] = jnp.zeros_like(note)

    def hidden_block(j):
        at = pl.ds(pl.multiple_of(j * BLOCK, BLOCK), BLOCK)
        low = (dot_nt(dq[0], wq[0, at, :]) + dot_nt(dq[1], wq[1, at, :])).astype(jnp.bfloat16)
        hp[j] = low
        product = low.astype(jnp.float32) * (xv[:, at].astype(jnp.float32) * inv[:, :1])
        gain = jnp.sum(product, axis=0, keepdims=True)
        product *= gain_ref[:, at]
        folded = product[:, :128]
        for b in range(8):
            gx[x, j, pl.ds(b, 1)] = gain[:, b * 128 : (b + 1) * 128]
            if b:
                folded += product[:, b * 128 : (b + 1) * 128]
        return folded

    def hidden_step(k, folded):
        j = (t + k) % 4
        folded += hidden_block(j)
        remote(hp.at[j], hp_in.at[t], h_send.at[0], h_recv.at[0], at_t(k)).start()
        return folded

    folded = lax.fori_loop(1, 4, hidden_step, jnp.zeros((ROWS, 128), jnp.float32))
    folded += hidden_block(t)
    for k in range(1, 4):
        remote(gx.at[x], gx.at[x], g_send.at[0], g_recv.at[0], at_x(k)).start()
    row = jnp.sum(folded.T, axis=0, keepdims=True)

    for h in range(HEADS_HERE):
        arrived(dkv.at[0, h], k_recv.at[0, h])

    def seq_rows(s, k, c):
        return pl.ds(pl.multiple_of(s * ROWS + (k * 2 + c) * 16, 16), 16)

    halves = [slice(0, COLS), slice(COLS, 2 * COLS)]
    for b, cols in enumerate(halves):
        for lane in (cols.start, cols.start + HEAD_DIM):
            at = slice(lane, lane + HEAD_DIM)
            de[:, at] += term(1, 1, at) + term(0, 0, at) + term(0, 1, at)
        for s in range(4):
            for k in range(4):
                de1[b, k, s] = de[seq_rows(s, k, 1 - core), cols].astype(jnp.bfloat16)
        remote(de1.at[b], de1_in.at[b], d_send.at[0, b], d_recv.at[0, b], other_core).start()

    arrived(gx, g_recv.at[0])
    for j in range(4):
        note[j, pl.ds(0, 1)] = row
        note[j, pl.ds(8, 8)] = gx[0, j] + gx[1, j] + gx[2, j] + gx[3, j]
    for k in range(1, 4):
        remote(
            note.at[(t + k) % 4], note_in.at[t], i_send.at[0], i_recv.at[0], at_t(k)
        ).start()

    for b, cols in enumerate(halves):
        wait_for(de1_in.at[b], d_recv.at[0, b])
        for k in range(1, 4):
            to = (y + k) % 4
            for s in range(4):
                de2[b, to, s] = (
                    de[seq_rows(s, to, core), cols] + de1_in[b, to, s].astype(jnp.float32)
                ).astype(jnp.bfloat16)
            remote(
                de2.at[b, to], de2_in.at[b, y], d_send.at[1, b], d_recv.at[1, b], at_y(k)
            ).start()

    for b, cols in enumerate(halves):
        arrived(de2_in.at[b], d_recv.at[1, b])
        for s in range(4):
            total = de[seq_rows(s, y, core), cols] + de1_in[b, y, s].astype(jnp.float32)
            for k in range(1, 4):
                total += de2_in[b, (y + k) % 4, s].astype(jnp.float32)
            dex[s, :, cols] = total.astype(jnp.bfloat16)
    for k in range(1, 4):
        remote(dex.at[(x + k) % 4], dex_in.at[x], d_send.at[2, 0], d_recv.at[2, 0], at_x(k)).start()

    arrived(note_in, i_recv.at[0])
    note_in[t] = note[t]
    noted = note_in[0] + note_in[1] + note_in[2] + note_in[3]
    gz[z] = noted[8:]
    for k in range(1, 4):
        remote(gz.at[z], gz.at[z], g_send.at[1], g_recv.at[1], at_z(k)).start()
    mean = jnp.broadcast_to(noted[:1] / D, (128, 128)).T[:, :1]

    arrived(dex_in, d_recv.at[2, 0])
    dex_in[x] = dex[x]
    stacked = jnp.concatenate([dex_in[b] for b in range(4)], axis=0)
    moved = regroup(stacked).astype(jnp.bfloat16)
    for b in range(4):
        de3[b] = moved[b * 16 : (b + 1) * 16]
    for k in range(1, 4):
        remote(
            de3.at[(t + k) % 4], de3_in.at[t], d_send.at[2, 1], d_recv.at[2, 1], at_t(k)
        ).start()

    og_load.wait()
    at = pl.ds(pl.multiple_of(t * BLOCK, BLOCK), BLOCK)
    scale_col = inv[:, :1]
    normed = xv[:, at].astype(jnp.float32) * scale_col
    arrived(hp_in, h_recv.at[0])
    hidden_grad = hp[t].astype(jnp.float32)
    for k in range(1, 4):
        hidden_grad += hp_in[(t + k) % 4].astype(jnp.float32)
    normed_grad = hidden_grad * gain_ref[:, at]
    ig_ref[0] = (
        og[...].astype(jnp.float32) + scale_col * (normed_grad - normed * mean)
    ).astype(jnp.bfloat16)

    arrived(gz, g_recv.at[1])
    gains = gz[0] + gz[1] + gz[2] + gz[3]
    for b in range(8):
        gg_ref[:, b * 128 : (b + 1) * 128] = gains[b : b + 1]

    arrived(de3_in, d_recv.at[2, 1])
    summed = de3[t].astype(jnp.float32)
    for k in range(1, 4):
        summed += de3_in[(t + k) % 4].astype(jnp.float32)
    lines[...] = summed
    for b in range(4):
        eg_ref[:, b * BLOCK : (b + 1) * BLOCK] = lines[pl.ds(b * 4, 4), :]

    for c in range(6):
        wait_bytes(z_send.at[c], 3 * SHARD)
    for h in range(HEADS_HERE):
        wait_bytes(x_send.at[h], 12 * SHARD)
        for m in range(2):
            arrived(part.at[m, h], p_send.at[m, h])
            arrived(dkv.at[m, h], k_send.at[m, h])
    wait_for(enc64.at[pl.ds(0, 48)], e_send.at[0])
    wait_for(enc.at[pl.ds(0, 48)], e_send.at[1])
    wait_for(enc.at[pl.ds(0, 192)], e_send.at[2])
    wait_for(enc.at[pl.ds(0, 256)], e_send.at[3])
    arrived(hp, h_send.at[0])
    arrived(note, i_send.at[0])
    for b in range(2):
        wait_for(de1.at[b], d_send.at[0, b])
        arrived(de2.at[b], d_send.at[1, b])
    arrived(dex, d_send.at[2, 0])
    arrived(de3, d_send.at[2, 1])
    arrived(gx, g_send.at[0])
    arrived(gz, g_send.at[1])


def shards(
    section_input, out_grad, head_grad, encoder, norm_gain, query_weight, key_weight, value_weight
):
    low, f32 = jnp.bfloat16, jnp.float32
    hbm = pl.BlockSpec(memory_space=pl.ANY)
    vmem = pl.BlockSpec(memory_space=pltpu.VMEM)
    dma = pltpu.SemaphoreType.DMA
    two = (2, HEADS_HERE)
    return pl.pallas_call(
        kernel,
        out_shape=(
            jax.ShapeDtypeStruct((1, ROWS, BLOCK), low),
            jax.ShapeDtypeStruct((4, D), f32),
            jax.ShapeDtypeStruct((1, BLOCK), f32),
        ),
        in_specs=[hbm, hbm, hbm, vmem, vmem, hbm, hbm, hbm],
        out_specs=(vmem, vmem, vmem),
        scratch_shapes=[
            pltpu.VMEM((HEADS_HERE, D, HEAD_DIM), low),
            pltpu.VMEM(two + (BLOCK, HEAD_DIM), low),
            pltpu.VMEM((ROWS, D), low),
            pltpu.VMEM((ROWS, BLOCK), low),
            pltpu.VMEM((ROWS, COLS), low),
            pltpu.VMEM((16, BLOCK), f32),
            pltpu.VMEM((64, BLOCK), low),
            pltpu.VMEM((4, 16, BLOCK), low),
            pltpu.VMEM((4 * ROWS, BLOCK), low),
            pltpu.VMEM((ROWS, D), low),
            pltpu.VMEM((ROWS, 128), f32),
            pltpu.VMEM(two + (4, ROWS, HEAD_DIM), low),
            pltpu.VMEM(two + (4, ROWS, HEAD_DIM), low),
            pltpu.VMEM(two + (ROWS, HEAD_DIM), low),
            pltpu.VMEM((HEADS_HERE, ROWS, HEAD_DIM), low),
            pltpu.VMEM((HEADS_HERE, ROWS, ROWS), f32),
            pltpu.VMEM((HEADS_HERE, ROWS, HEAD_DIM), low),
            pltpu.VMEM(two + (4, ROWS, HEAD_DIM), low),
            pltpu.VMEM((4, ROWS, BLOCK), low),
            pltpu.VMEM((4, ROWS, BLOCK), low),
            pltpu.VMEM((4, 16, 128), f32),
            pltpu.VMEM((4, 16, 128), f32),
            pltpu.VMEM((4 * ROWS, BLOCK), f32),
            pltpu.VMEM((2, 4, 4, 16, COLS), low),
            pltpu.VMEM((2, 4, 4, 16, COLS), low),
            pltpu.VMEM((2, 4, 4, 16, COLS), low),
            pltpu.VMEM((2, 4, 4, 16, COLS), low),
            pltpu.VMEM((4, 16, BLOCK), low),
            pltpu.VMEM((4, 16, BLOCK), low),
            pltpu.VMEM((4, 16, BLOCK), low),
            pltpu.VMEM((4, 16, BLOCK), low),
            pltpu.VMEM((4, 8, 128), f32),
            pltpu.VMEM((4, 4, 8, 128), f32),
            dma((10,)),
            dma((6,)),
            dma((HEADS_HERE,)),
            dma((6,)),
            dma((6,)),
            dma((4, HEADS_HERE)),
            dma((4, HEADS_HERE)),
            dma(two),
            dma(two),
            dma(two),
            dma(two),
            dma((4,)),
            dma((4,)),
            dma((1,)),
            dma((1,)),
            dma((1,)),
            dma((1,)),
            dma((3, 2)),
            dma((3, 2)),
            dma((2,)),
            dma((2,)),
        ],
        compiler_params=pltpu.CompilerParams(
            collective_id=0, has_side_effects=True, vmem_limit_bytes=60 * 1024 * 1024
        ),
        cost_estimate=pl.CostEstimate(
            flops=6 * 2 * ROWS * D * COLS, bytes_accessed=4 * 1024 * 1024, transcendentals=0
        ),
    )(
        section_input, out_grad, head_grad, encoder, norm_gain,
        query_weight, key_weight, value_weight,
    )


def solution(mesh):
    placed = (
        P("pipe", "dp", None),
        P("pipe", "dp", None),
        P("pipe", "dp", "tensor"),
        P(("dp", "pipe", "tensor"), None),
        P("pipe", None),
        P("pipe", "dp", "tensor"),
        P("pipe", "dp", "tensor"),
        P("pipe", "dp", "tensor"),
    )
    return jax.shard_map(
        shards,
        mesh=mesh,
        in_specs=placed,
        out_specs=(
            P("pipe", "dp", "tensor"),
            P(("dp", "pipe", "tensor"), None),
            P("pipe", "tensor"),
        ),
        check_vma=False,
    )
```

```python
import math

import jax
import jax.numpy as jnp
from jax import lax
from jax.experimental import pallas as pl
from jax.experimental.pallas import tpu as pltpu
from jax.sharding import PartitionSpec as P

HEAD_DIM = 256
HEADS_HERE = 2
COLS = 512
D = 4096
ROWS = 128
SHARD = 256
HALF = SHARD // 2
BLOCK = 1024
EPSILON = 1e-06
MESH = pl.DeviceIdType.MESH
QUARTER = SHARD // 4
PIECES = [
    (0, 0, 0, SHARD), (0, 1, 0, SHARD), (1, 0, 0, SHARD), (1, 1, 0, SHARD), (2, 0, 0, SHARD),
    (2, 1, 0, HALF), (2, 1, HALF, HALF),
]


def dot_nt(left, right):
    return lax.dot_general(
        left, right, (((1,), (1,)), ((), ())), preferred_element_type=jnp.float32
    )


def dot_tn(left, right):
    return lax.dot_general(
        left, right, (((0,), (0,)), ((), ())), preferred_element_type=jnp.float32
    )


def regroup(rows):
    i = lax.broadcasted_iota(jnp.int32, (64, 64), 0)
    j = lax.broadcasted_iota(jnp.int32, (64, 64), 1)
    source = (i % 16) // 4 * 16 + i // 16 * 4 + i % 4
    hot = jnp.where(j == source, 1.0, 0.0).astype(jnp.bfloat16)
    return jnp.dot(hot, rows, preferred_element_type=jnp.float32)


def kernel(
    x_hbm, og_hbm, hg_hbm, enc_ref, gain_ref, wq_hbm, wk_hbm, wv_hbm,
    ig_ref, eg_ref, gg_ref,
    wq, wkv, xv, og, hg, lines, enc64, encx, enc, hid, inv, part, part_in, kv, qb, probs, dq, dkv,
    hp, hp_in, note, note_in, de, de1, de1_in, de2, de2_in, de3, de3_in, gz, gz_in, gx,
    local, z_send, x_send, z_near, z_far, x_near, x_far, p_send, p_recv, k_send, k_recv,
    e_send, e_recv, h_send, h_recv, i_send, i_recv, d_send, d_recv, g_send, g_recv,
):
    dp = lax.axis_index("dp")
    pipe = lax.axis_index("pipe")
    t = lax.axis_index("tensor")
    x, z = dp // 4, dp % 4
    y, core = pipe // 2, pipe % 2

    def at_z(k):
        return (x * 4 + (z + k) % 4, pipe, t)

    def at_x(k):
        return ((x + k) % 4 * 4 + z, pipe, t)

    def at_y(k):
        return (dp, (y + k) % 4 * 2 + core, t)

    def at_t(k):
        return (dp, pipe, (t + k) % 4)

    def at_line(k):
        to = (z * 4 + t + k) % 16
        return (x * 4 + to // 4, pipe, to % 4)

    def at_plane(k):
        to = (x * 4 + t + k) % 16
        return (to // 4 * 4 + z, pipe, to % 4)

    other_core = (dp, y * 2 + 1 - core, t)

    def remote(src, dst, send, recv, peer):
        return pltpu.make_async_remote_copy(
            src_ref=src, dst_ref=dst, send_sem=send, recv_sem=recv,
            device_id=peer, device_id_type=MESH,
        )

    def rows_of(ref, block, rows, start=0):
        return ref.at[pl.ds(pl.multiple_of(block * rows + start, 16), rows)]

    def wait_for(ref, sem):
        pltpu.make_async_copy(ref, ref, sem).wait()

    def arrived(ref, sem):
        wait_for(ref.at[pl.ds(0, 3)], sem)

    def piece(c, xx, zz, start=0, rows=None):
        m, h, first_row, count = PIECES[c]
        start, rows = start + first_row, rows or count
        if m == 0:
            first = (xx * 4 + zz) * SHARD + start
            return wq.at[h, pl.ds(pl.multiple_of(first, QUARTER), rows)]
        return wkv.at[m - 1, h, pl.ds(pl.multiple_of(zz * SHARD + start, QUARTER), rows)]

    sources = (wq_hbm, wk_hbm, wv_hbm)
    loads = [
        pltpu.make_async_copy(
            sources[m].at[0, pl.ds(start, rows), pl.ds(h * HEAD_DIM, HEAD_DIM)],
            piece(c, x, z), local.at[c],
        )
        for c, (m, h, start, rows) in enumerate(PIECES)
    ]
    x_load = pltpu.make_async_copy(x_hbm.at[0], xv, local.at[8])
    hg_load = pltpu.make_async_copy(hg_hbm.at[0], hg, local.at[9])
    og_load = pltpu.make_async_copy(
        og_hbm.at[0, :, pl.ds(pl.multiple_of(t * BLOCK, BLOCK), BLOCK)], og, local.at[10]
    )
    for copy in loads + [x_load, hg_load, og_load]:
        copy.start()

    barrier = pltpu.get_barrier_semaphore()
    peers = [at_line(k) for k in range(1, 16)] + [other_core]
    for k in range(1, 4):
        peers += [at_y(k)] + [((x + k) % 4 * 4 + z, pipe, b) for b in range(4)]
    for peer in peers:
        pl.semaphore_signal(barrier, inc=1, device_id=peer, device_id_type=MESH)
    for b in range(4):
        lines[pl.ds(b * 4, 4), :] = enc_ref[:, b * BLOCK : (b + 1) * BLOCK].astype(jnp.float32)
    enc64[pl.ds(pl.multiple_of(t * 16, 16), 16), :] = lines[...].astype(jnp.bfloat16)
    for copy in loads:
        copy.wait()
    pl.semaphore_wait(barrier, len(peers))

    def wait_bytes(sem, rows):
        wait_for(wq.at[0, pl.ds(0, rows)], sem)

    def z_first(c):
        own = piece(c, x, z)
        for k in (1, -1):
            remote(own, own, z_send.at[c], z_near.at[c], at_z(k)).start()

    def z_second(c):
        rows = PIECES[c][3]
        wait_bytes(z_near.at[c], 2 * rows)
        up = piece(c, x, (z + 3) % 4, rows // 2, rows // 2)
        remote(up, up, z_send.at[c], z_far.at[c], at_z(1)).start()
        down = piece(c, x, (z + 1) % 4, 0, rows // 2)
        remote(down, down, z_send.at[c], z_far.at[c], at_z(-1)).start()

    def x_first(h, j):
        own = piece(h, x, (z + j) % 4)
        for k in (1, -1):
            remote(own, own, x_send.at[h], x_near.at[j, h], at_x(k)).start()

    def x_second(h, j):
        wait_bytes(x_near.at[j, h], 2 * SHARD)
        up = piece(h, (x + 3) % 4, (z + j) % 4, HALF, HALF)
        remote(up, up, x_send.at[h], x_far.at[j, h], at_x(1)).start()
        down = piece(h, (x + 1) % 4, (z + j) % 4, 0, HALF)
        remote(down, down, x_send.at[h], x_far.at[j, h], at_x(-1)).start()

    own16 = rows_of(enc64, t, 16)
    for k in range(1, 4):
        remote(own16, own16, e_send.at[0], e_recv.at[0], at_t(k)).start()
    z_first(0)
    z_first(1)
    x_first(0, 0)
    x_first(1, 0)

    def enc_x():
        wait_for(enc64.at[pl.ds(0, 48)], e_recv.at[0])
        moved = regroup(enc64[...]).astype(jnp.bfloat16)
        for b in range(4):
            encx[b] = moved[b * 16 : (b + 1) * 16]
        enc[pl.ds(pl.multiple_of(pipe * 64 + x * 16, 16), 16), :] = encx[x]
        for k in range(1, 4):
            remote(
                encx.at[(x + k) % 4],
                enc.at[pl.ds(pl.multiple_of(pipe * 64 + x * 16, 16), 16)],
                e_send.at[1], e_recv.at[1], at_x(k),
            ).start()

    def enc_y():
        wait_for(enc.at[pl.ds(0, 48)], e_recv.at[1])
        mine = rows_of(enc, pipe, 64)
        for k in range(1, 4):
            remote(mine, mine, e_send.at[2], e_recv.at[2], at_y(k)).start()

    def enc_core():
        wait_for(enc.at[pl.ds(0, 192)], e_recv.at[2])
        for k in range(4):
            mine = rows_of(enc, k * 2 + core, 64)
            remote(mine, mine, e_send.at[3], e_recv.at[3], other_core).start()

    def norm():
        x_load.wait()
        total = jnp.zeros((ROWS, 1), jnp.float32)
        for b in range(4):
            block = xv[:, b * BLOCK : (b + 1) * BLOCK].astype(jnp.float32)
            total += jnp.sum(block * block, axis=1, keepdims=True)
        scale = lax.rsqrt(total / D + EPSILON)
        inv[...] = jnp.broadcast_to(scale, (ROWS, 128))
        for b in range(4):
            cols = slice(b * BLOCK, (b + 1) * BLOCK)
            normed = xv[:, cols].astype(jnp.float32) * scale
            hid[:, cols] = (normed * gain_ref[:, cols]).astype(jnp.bfloat16)

    def share(m, h):
        for c, (weight, head, _, rows) in enumerate(PIECES):
            if (weight, head) == (m + 1, h):
                wait_bytes(z_far.at[c], rows)
        rows = jnp.dot(enc[...], wkv[m, h], preferred_element_type=jnp.float32).astype(jnp.bfloat16)
        for p in range(8):
            for b in range(4):
                part[m, h, b, pl.ds(p * 16, 16), :] = rows[p * 64 + b * 16 : p * 64 + (b + 1) * 16]
        for k in range(1, 4):
            remote(
                part.at[m, h, (x + k) % 4], part_in.at[m, h, x],
                p_send.at[m, h], p_recv.at[m, h], at_x(k),
            ).start()

    def combine(m, h):
        arrived(part_in.at[m, h], p_recv.at[m, h])
        total = part[m, h, x].astype(jnp.float32)
        for k in range(1, 4):
            total += part_in[m, h, (x + k) % 4].astype(jnp.float32)
        kv[m, h] = total.astype(jnp.bfloat16)

    scale = 1.0 / math.sqrt(HEAD_DIM)

    def spread(m, h, grad):
        dkv[m, h, x] = grad.astype(jnp.bfloat16)
        mine = dkv.at[m, h, x]
        for k in range(1, 4):
            remote(mine, mine, k_send.at[m, h], k_recv.at[m, h], at_x(k)).start()

    def queries(h):
        for j in range(4):
            wait_bytes(x_far.at[j, h], SHARD)
        total = jnp.zeros((ROWS, HEAD_DIM), jnp.float32)

        def add(k, total):
            at = pl.ds(pl.multiple_of(k * BLOCK, BLOCK), BLOCK)
            return total + jnp.dot(hid[:, at], wq[h, at, :], preferred_element_type=jnp.float32)

        qb[h] = lax.fori_loop(0, 4, add, total).astype(jnp.bfloat16)

    def soften(h):
        expo = jnp.exp(dot_nt(qb[h], kv[0, h]) * scale)
        soft = expo / jnp.sum(expo, axis=1, keepdims=True)
        probs[h] = soft
        head = hg[:, h * HEAD_DIM : (h + 1) * HEAD_DIM]
        spread(1, h, dot_tn(soft.astype(jnp.bfloat16), head))

    def attend(h):
        soft = probs[h]
        prob_grad = dot_nt(hg[:, h * HEAD_DIM : (h + 1) * HEAD_DIM], kv[1, h])
        mean = jnp.sum(prob_grad * soft, axis=1, keepdims=True)
        score_grad = (soft * (prob_grad - mean) * scale).astype(jnp.bfloat16)
        spread(0, h, dot_tn(score_grad, qb[h]))
        dq[h] = jnp.dot(score_grad, kv[0, h], preferred_element_type=jnp.float32).astype(
            jnp.bfloat16
        )

    def term(m, h, cols):
        left = dkv[m, h].reshape(4 * ROWS, HEAD_DIM)
        return dot_nt(left, wkv[m, h, cols, :])

    def early_encoder():
        arrived(dkv.at[1, 0], k_recv.at[1, 0])
        arrived(dkv.at[1, 1], k_recv.at[1, 1])

        @pl.loop(0, 4)
        def _(b):
            at = pl.ds(pl.multiple_of(b * HEAD_DIM, HEAD_DIM), HEAD_DIM)
            de[:, at] = term(1, 0, at)

    z_second(0)
    z_first(2)
    x_first(0, 1)
    x_first(0, 3)
    enc_x()
    norm()
    x_second(0, 0)
    x_second(1, 0)

    z_second(1)
    z_first(3)
    x_first(1, 1)
    x_first(1, 3)
    enc_y()
    wait_bytes(z_far.at[0], SHARD)
    x_first(0, 2)
    x_second(0, 1)
    x_second(0, 3)

    z_second(2)
    z_first(4)
    enc_core()
    wait_bytes(z_far.at[1], SHARD)
    x_first(1, 2)
    x_second(0, 2)
    x_second(1, 1)
    x_second(1, 3)

    z_second(3)
    z_first(5)
    z_first(6)
    x_second(1, 2)
    wait_for(enc.at[pl.ds(0, 256)], e_recv.at[3])
    share(0, 0)
    queries(0)
    queries(1)
    hg_load.wait()

    z_second(4)
    combine(0, 0)
    soften(0)

    z_second(5)
    share(0, 1)
    z_second(6)
    share(1, 0)
    combine(0, 1)
    soften(1)

    share(1, 1)
    combine(1, 0)
    attend(0)
    early_encoder()
    combine(1, 1)
    attend(1)

    def hidden_block(j):
        at = pl.ds(pl.multiple_of(j * BLOCK, BLOCK), BLOCK)
        low = (dot_nt(dq[0], wq[0, at, :]) + dot_nt(dq[1], wq[1, at, :])).astype(jnp.bfloat16)
        hp[j] = low
        product = low.astype(jnp.float32) * (xv[:, at].astype(jnp.float32) * inv[:, :1])
        gain = jnp.sum(product, axis=0, keepdims=True)
        product *= gain_ref[:, at]
        folded = product[:, :128]
        for b in range(8):
            gx[x, j, pl.ds(b, 1)] = gain[:, b * 128 : (b + 1) * 128]
            if b:
                folded += product[:, b * 128 : (b + 1) * 128]
        return folded

    def hidden_step(k, folded):
        j = (t + k) % 4
        folded += hidden_block(j)
        remote(hp.at[j], hp_in.at[t], h_send.at[0], h_recv.at[0], at_t(k)).start()
        return folded

    folded = lax.fori_loop(1, 4, hidden_step, jnp.zeros((ROWS, 128), jnp.float32))
    folded += hidden_block(t)
    for k in range(1, 4):
        remote(gx.at[x], gx.at[x], g_send.at[0], g_recv.at[0], at_x(k)).start()
    row = jnp.sum(folded.T, axis=0, keepdims=True)
    note[...] = jnp.broadcast_to(row, (8, 128))
    for k in range(1, 4):
        remote(note, note_in.at[t], i_send.at[0], i_recv.at[0], at_t(k)).start()

    for h in range(HEADS_HERE):
        arrived(dkv.at[0, h], k_recv.at[0, h])

    def seq_rows(s, k, c):
        return pl.ds(pl.multiple_of(s * ROWS + (k * 2 + c) * 16, 16), 16)

    halves = [slice(0, COLS), slice(COLS, 2 * COLS)]
    for b, cols in enumerate(halves):
        for lane in (cols.start, cols.start + HEAD_DIM):
            at = slice(lane, lane + HEAD_DIM)
            de[:, at] += term(1, 1, at) + term(0, 0, at) + term(0, 1, at)
        for s in range(4):
            for k in range(4):
                de1[b, k, s] = de[seq_rows(s, k, 1 - core), cols].astype(jnp.bfloat16)
        remote(de1.at[b], de1_in.at[b], d_send.at[0, b], d_recv.at[0, b], other_core).start()

    arrived(gx, g_recv.at[0])
    for j in range(4):
        gz[j] = gx[0, j] + gx[1, j] + gx[2, j] + gx[3, j]
    for k in range(1, 16):
        remote(
            gz.at[(t + k) % 4], gz_in.at[z * 4 + t], g_send.at[1], g_recv.at[1], at_line(k)
        ).start()

    for b, cols in enumerate(halves):
        wait_for(de1_in.at[b], d_recv.at[0, b])
        for k in range(1, 4):
            to = (y + k) % 4
            for s in range(4):
                de2[b, to, s] = (
                    de[seq_rows(s, to, core), cols] + de1_in[b, to, s].astype(jnp.float32)
                ).astype(jnp.bfloat16)
            remote(
                de2.at[b, to], de2_in.at[b, y], d_send.at[1, b], d_recv.at[1, b], at_y(k)
            ).start()

    quarters = [[] for _ in range(4)]
    for b, cols in enumerate(halves):
        arrived(de2_in.at[b], d_recv.at[1, b])
        for s in range(4):
            total = de[seq_rows(s, y, core), cols] + de1_in[b, y, s].astype(jnp.float32)
            for k in range(1, 4):
                total += de2_in[b, (y + k) % 4, s].astype(jnp.float32)
            low = total.astype(jnp.bfloat16)
            quarters[s] += [low[:, :HEAD_DIM], low[:, HEAD_DIM:]]
    stacked = jnp.concatenate([jnp.concatenate(q, axis=0) for q in quarters], axis=1)
    moved = regroup(stacked).astype(jnp.bfloat16)
    for s in range(4):
        for b in range(4):
            de3[s * 4 + b] = moved[b * 16 : (b + 1) * 16, s * HEAD_DIM : (s + 1) * HEAD_DIM]
    for k in range(1, 16):
        remote(
            de3.at[(x * 4 + t + k) % 16], de3_in.at[x * 4 + t],
            d_send.at[2, 0], d_recv.at[2, 0], at_plane(k),
        ).start()

    og_load.wait()
    at = pl.ds(pl.multiple_of(t * BLOCK, BLOCK), BLOCK)
    scale_col = inv[:, :1]
    normed = xv[:, at].astype(jnp.float32) * scale_col
    arrived(note_in, i_recv.at[0])
    note_in[t] = note[...]
    noted = note_in[0] + note_in[1] + note_in[2] + note_in[3]
    mean = jnp.broadcast_to(noted[:1] / D, (128, 128)).T[:, :1]
    arrived(hp_in, h_recv.at[0])
    hidden_grad = hp[t].astype(jnp.float32)
    for k in range(1, 4):
        hidden_grad += hp_in[(t + k) % 4].astype(jnp.float32)
    normed_grad = hidden_grad * gain_ref[:, at]
    ig_ref[0] = (
        og[...].astype(jnp.float32) + scale_col * (normed_grad - normed * mean)
    ).astype(jnp.bfloat16)

    wait_for(gz_in.at[pl.ds(0, 15)], g_recv.at[1])
    gz_in[z * 4 + t] = gz[t]
    gains = gz_in[0]
    for k in range(1, 16):
        gains += gz_in[k]
    for b in range(8):
        gg_ref[:, b * 128 : (b + 1) * 128] = gains[b : b + 1]

    wait_for(de3_in.at[pl.ds(0, 15)], d_recv.at[2, 0])
    de3_in[x * 4 + t] = de3[x * 4 + t]
    for b in range(4):
        summed = de3_in[b * 4].astype(jnp.float32)
        for k in range(1, 4):
            summed += de3_in[b * 4 + k].astype(jnp.float32)
        lines[:, b * HEAD_DIM : (b + 1) * HEAD_DIM] = summed
    for b in range(4):
        for k in range(4):
            eg_ref[:, b * BLOCK + k * HEAD_DIM : b * BLOCK + (k + 1) * HEAD_DIM] = lines[
                pl.ds(k * 4, 4), b * HEAD_DIM : (b + 1) * HEAD_DIM
            ]

    for c in range(len(PIECES)):
        wait_bytes(z_send.at[c], 3 * PIECES[c][3])
    for h in range(HEADS_HERE):
        wait_bytes(x_send.at[h], 12 * SHARD)
        for m in range(2):
            arrived(part.at[m, h], p_send.at[m, h])
            arrived(dkv.at[m, h], k_send.at[m, h])
    wait_for(enc64.at[pl.ds(0, 48)], e_send.at[0])
    wait_for(enc.at[pl.ds(0, 48)], e_send.at[1])
    wait_for(enc.at[pl.ds(0, 192)], e_send.at[2])
    wait_for(enc.at[pl.ds(0, 256)], e_send.at[3])
    arrived(hp, h_send.at[0])
    arrived(note_in, i_send.at[0])
    for b in range(2):
        wait_for(de1.at[b], d_send.at[0, b])
        arrived(de2.at[b], d_send.at[1, b])
    wait_for(de3.at[pl.ds(0, 15)], d_send.at[2, 0])
    arrived(gx, g_send.at[0])
    wait_for(gz_in.at[pl.ds(0, 15)], g_send.at[1])


def shards(
    section_input, out_grad, head_grad, encoder, norm_gain, query_weight, key_weight, value_weight
):
    low, f32 = jnp.bfloat16, jnp.float32
    hbm = pl.BlockSpec(memory_space=pl.ANY)
    vmem = pl.BlockSpec(memory_space=pltpu.VMEM)
    dma = pltpu.SemaphoreType.DMA
    two = (2, HEADS_HERE)
    return pl.pallas_call(
        kernel,
        out_shape=(
            pltpu.VMEM((1, ROWS, BLOCK), low),
            pltpu.VMEM((4, D), f32),
            pltpu.VMEM((1, BLOCK), f32),
        ),
        in_specs=[hbm, hbm, hbm, vmem, vmem, hbm, hbm, hbm],
        out_specs=(vmem, vmem, vmem),
        scratch_shapes=[
            pltpu.VMEM((HEADS_HERE, D, HEAD_DIM), low),
            pltpu.VMEM(two + (BLOCK, HEAD_DIM), low),
            pltpu.VMEM((ROWS, D), low),
            pltpu.VMEM((ROWS, BLOCK), low),
            pltpu.VMEM((ROWS, COLS), low),
            pltpu.VMEM((16, BLOCK), f32),
            pltpu.VMEM((64, BLOCK), low),
            pltpu.VMEM((4, 16, BLOCK), low),
            pltpu.VMEM((4 * ROWS, BLOCK), low),
            pltpu.VMEM((ROWS, D), low),
            pltpu.VMEM((ROWS, 128), f32),
            pltpu.VMEM(two + (4, ROWS, HEAD_DIM), low),
            pltpu.VMEM(two + (4, ROWS, HEAD_DIM), low),
            pltpu.VMEM(two + (ROWS, HEAD_DIM), low),
            pltpu.VMEM((HEADS_HERE, ROWS, HEAD_DIM), low),
            pltpu.VMEM((HEADS_HERE, ROWS, ROWS), f32),
            pltpu.VMEM((HEADS_HERE, ROWS, HEAD_DIM), low),
            pltpu.VMEM(two + (4, ROWS, HEAD_DIM), low),
            pltpu.VMEM((4, ROWS, BLOCK), low),
            pltpu.VMEM((4, ROWS, BLOCK), low),
            pltpu.VMEM((8, 128), f32),
            pltpu.VMEM((4, 8, 128), f32),
            pltpu.VMEM((4 * ROWS, BLOCK), f32),
            pltpu.VMEM((2, 4, 4, 16, COLS), low),
            pltpu.VMEM((2, 4, 4, 16, COLS), low),
            pltpu.VMEM((2, 4, 4, 16, COLS), low),
            pltpu.VMEM((2, 4, 4, 16, COLS), low),
            pltpu.VMEM((16, 16, HEAD_DIM), low),
            pltpu.VMEM((16, 16, HEAD_DIM), low),
            pltpu.VMEM((4, 8, 128), f32),
            pltpu.VMEM((16, 8, 128), f32),
            pltpu.VMEM((4, 4, 8, 128), f32),
            dma((11,)),
            dma((len(PIECES),)),
            dma((HEADS_HERE,)),
            dma((len(PIECES),)),
            dma((len(PIECES),)),
            dma((4, HEADS_HERE)),
            dma((4, HEADS_HERE)),
            dma(two),
            dma(two),
            dma(two),
            dma(two),
            dma((4,)),
            dma((4,)),
            dma((1,)),
            dma((1,)),
            dma((1,)),
            dma((1,)),
            dma((3, 2)),
            dma((3, 2)),
            dma((2,)),
            dma((2,)),
        ],
        compiler_params=pltpu.CompilerParams(
            collective_id=0, has_side_effects=True, vmem_limit_bytes=60 * 1024 * 1024
        ),
        cost_estimate=pl.CostEstimate(
            flops=6 * 2 * ROWS * D * COLS, bytes_accessed=4 * 1024 * 1024, transcendentals=0
        ),
    )(
        section_input, out_grad, head_grad, encoder, norm_gain,
        query_weight, key_weight, value_weight,
    )


def solution(mesh):
    placed = (
        P("pipe", "dp", None),
        P("pipe", "dp", None),
        P("pipe", "dp", "tensor"),
        P(("dp", "pipe", "tensor"), None),
        P("pipe", None),
        P("pipe", "dp", "tensor"),
        P("pipe", "dp", "tensor"),
        P("pipe", "dp", "tensor"),
    )
    return jax.shard_map(
        shards,
        mesh=mesh,
        in_specs=placed,
        out_specs=(
            P("pipe", "dp", "tensor"),
            P(("dp", "pipe", "tensor"), None),
            P("pipe", "tensor"),
        ),
        check_vma=False,
    )
```

```python
import math

import jax
import jax.numpy as jnp
from jax import lax
from jax.experimental import pallas as pl
from jax.experimental.pallas import tpu as pltpu
from jax.sharding import PartitionSpec as P

HEAD_DIM = 256
HEADS_HERE = 2
COLS = 512
D = 4096
ROWS = 128
SHARD = 256
HALF = SHARD // 2
BLOCK = 1024
EPSILON = 1e-06
MESH = pl.DeviceIdType.MESH
QUARTER = SHARD // 4
PIECES = [
    (0, 0, 0, SHARD), (0, 1, 0, SHARD), (1, 0, 0, SHARD), (1, 1, 0, SHARD), (2, 0, 0, SHARD),
    (2, 1, 0, HALF), (2, 1, HALF, HALF),
]


def dot_nt(left, right):
    return lax.dot_general(
        left, right, (((1,), (1,)), ((), ())), preferred_element_type=jnp.float32
    )


def dot_tn(left, right):
    return lax.dot_general(
        left, right, (((0,), (0,)), ((), ())), preferred_element_type=jnp.float32
    )


def regroup(rows):
    i = lax.broadcasted_iota(jnp.int32, (64, 64), 0)
    j = lax.broadcasted_iota(jnp.int32, (64, 64), 1)
    source = (i % 16) // 4 * 16 + i // 16 * 4 + i % 4
    hot = jnp.where(j == source, 1.0, 0.0).astype(jnp.bfloat16)
    return jnp.dot(hot, rows, preferred_element_type=jnp.float32)


def kernel(
    x_hbm, og_hbm, hg_hbm, enc_ref, gain_ref, wq_hbm, wk_hbm, wv_hbm,
    ig_ref, eg_ref, gg_ref,
    wq, wkv, xv, og, hg, lines, enc64, encx, enc, hid, inv, part, part_in, kv, qb, probs, dq, dkv,
    hp, hp_in, hp_out, note, note_in, de, de1, de1_in, de2, de2_in, de3, de3_in, gz, gx,
    local, z_send, x_send, z_near, z_far, x_near, x_far, p_send, p_recv, k_send, k_recv,
    e_send, e_recv, h_send, h_recv, i_send, i_recv, d_send, d_recv, g_send, g_recv,
):
    dp = lax.axis_index("dp")
    pipe = lax.axis_index("pipe")
    t = lax.axis_index("tensor")
    x, z = dp // 4, dp % 4
    y, core = pipe // 2, pipe % 2

    def at_z(k):
        return (x * 4 + (z + k) % 4, pipe, t)

    def at_x(k):
        return ((x + k) % 4 * 4 + z, pipe, t)

    def at_y(k):
        return (dp, (y + k) % 4 * 2 + core, t)

    def at_t(k):
        return (dp, pipe, (t + k) % 4)

    def at_plane(k):
        to = (x * 4 + t + k) % 16
        return (to // 4 * 4 + z, pipe, to % 4)

    other_core = (dp, y * 2 + 1 - core, t)

    def remote(src, dst, send, recv, peer):
        return pltpu.make_async_remote_copy(
            src_ref=src, dst_ref=dst, send_sem=send, recv_sem=recv,
            device_id=peer, device_id_type=MESH,
        )

    def rows_of(ref, block, rows, start=0):
        return ref.at[pl.ds(pl.multiple_of(block * rows + start, 16), rows)]

    def wait_for(ref, sem):
        pltpu.make_async_copy(ref, ref, sem).wait()

    def arrived(ref, sem):
        wait_for(ref.at[pl.ds(0, 3)], sem)

    def piece(c, xx, zz, start=0, rows=None):
        m, h, first_row, count = PIECES[c]
        start, rows = start + first_row, rows or count
        if m == 0:
            first = (xx * 4 + zz) * SHARD + start
            return wq.at[h, pl.ds(pl.multiple_of(first, QUARTER), rows)]
        return wkv.at[m - 1, h, pl.ds(pl.multiple_of(zz * SHARD + start, QUARTER), rows)]

    sources = (wq_hbm, wk_hbm, wv_hbm)
    loads = [
        pltpu.make_async_copy(
            sources[m].at[0, pl.ds(start, rows), pl.ds(h * HEAD_DIM, HEAD_DIM)],
            piece(c, x, z), local.at[c],
        )
        for c, (m, h, start, rows) in enumerate(PIECES)
    ]
    x_load = pltpu.make_async_copy(x_hbm.at[0], xv, local.at[8])
    hg_load = pltpu.make_async_copy(hg_hbm.at[0], hg, local.at[9])
    og_load = pltpu.make_async_copy(
        og_hbm.at[0, :, pl.ds(pl.multiple_of(t * BLOCK, BLOCK), BLOCK)], og, local.at[10]
    )
    for copy in loads + [x_load, hg_load, og_load]:
        copy.start()

    barrier = pltpu.get_barrier_semaphore()
    peers = [other_core]
    for k in range(1, 4):
        peers += [at_z(k), at_t(k), at_y(k)] + [((x + k) % 4 * 4 + z, pipe, b) for b in range(4)]
    for peer in peers:
        pl.semaphore_signal(barrier, inc=1, device_id=peer, device_id_type=MESH)
    for b in range(4):
        lines[pl.ds(b * 4, 4), :] = enc_ref[:, b * BLOCK : (b + 1) * BLOCK].astype(jnp.float32)
    enc64[pl.ds(pl.multiple_of(t * 16, 16), 16), :] = lines[...].astype(jnp.bfloat16)
    for copy in loads:
        copy.wait()
    pl.semaphore_wait(barrier, len(peers))

    def wait_bytes(sem, rows):
        wait_for(wq.at[0, pl.ds(0, rows)], sem)

    def z_first(c):
        own = piece(c, x, z)
        for k in (1, -1):
            remote(own, own, z_send.at[c], z_near.at[c], at_z(k)).start()

    def z_second(c):
        rows = PIECES[c][3]
        wait_bytes(z_near.at[c], 2 * rows)
        up = piece(c, x, (z + 3) % 4, rows // 2, rows // 2)
        remote(up, up, z_send.at[c], z_far.at[c], at_z(1)).start()
        down = piece(c, x, (z + 1) % 4, 0, rows // 2)
        remote(down, down, z_send.at[c], z_far.at[c], at_z(-1)).start()

    def x_first(h, j):
        own = piece(h, x, (z + j) % 4)
        for k in (1, -1):
            remote(own, own, x_send.at[h], x_near.at[j, h], at_x(k)).start()

    def x_second(h, j):
        wait_bytes(x_near.at[j, h], 2 * SHARD)
        up = piece(h, (x + 3) % 4, (z + j) % 4, HALF, HALF)
        remote(up, up, x_send.at[h], x_far.at[j, h], at_x(1)).start()
        down = piece(h, (x + 1) % 4, (z + j) % 4, 0, HALF)
        remote(down, down, x_send.at[h], x_far.at[j, h], at_x(-1)).start()

    own16 = rows_of(enc64, t, 16)
    for k in range(1, 4):
        remote(own16, own16, e_send.at[0], e_recv.at[0], at_t(k)).start()
    z_first(0)
    z_first(1)
    x_first(0, 0)
    x_first(1, 0)

    def enc_x():
        wait_for(enc64.at[pl.ds(0, 48)], e_recv.at[0])
        moved = regroup(enc64[...]).astype(jnp.bfloat16)
        for b in range(4):
            encx[b] = moved[b * 16 : (b + 1) * 16]
        enc[pl.ds(pl.multiple_of(pipe * 64 + x * 16, 16), 16), :] = encx[x]
        for k in range(1, 4):
            remote(
                encx.at[(x + k) % 4],
                enc.at[pl.ds(pl.multiple_of(pipe * 64 + x * 16, 16), 16)],
                e_send.at[1], e_recv.at[1], at_x(k),
            ).start()

    def enc_y():
        wait_for(enc.at[pl.ds(0, 48)], e_recv.at[1])
        mine = rows_of(enc, pipe, 64)
        for k in range(1, 4):
            remote(mine, mine, e_send.at[2], e_recv.at[2], at_y(k)).start()

    def enc_core():
        wait_for(enc.at[pl.ds(0, 192)], e_recv.at[2])
        for k in range(4):
            mine = rows_of(enc, k * 2 + core, 64)
            remote(mine, mine, e_send.at[3], e_recv.at[3], other_core).start()

    def norm():
        x_load.wait()
        total = jnp.zeros((ROWS, 1), jnp.float32)
        for b in range(4):
            block = xv[:, b * BLOCK : (b + 1) * BLOCK].astype(jnp.float32)
            total += jnp.sum(block * block, axis=1, keepdims=True)
        scale = lax.rsqrt(total / D + EPSILON)
        inv[...] = jnp.broadcast_to(scale, (ROWS, 128))
        for b in range(4):
            cols = slice(b * BLOCK, (b + 1) * BLOCK)
            normed = xv[:, cols].astype(jnp.float32) * scale
            hid[:, cols] = (normed * gain_ref[:, cols]).astype(jnp.bfloat16)

    def share(m, h):
        for c, (weight, head, _, rows) in enumerate(PIECES):
            if (weight, head) == (m + 1, h):
                wait_bytes(z_far.at[c], rows)
        rows = jnp.dot(enc[...], wkv[m, h], preferred_element_type=jnp.float32).astype(jnp.bfloat16)
        for p in range(8):
            for b in range(4):
                part[m, h, b, pl.ds(p * 16, 16), :] = rows[p * 64 + b * 16 : p * 64 + (b + 1) * 16]
        for k in range(1, 4):
            remote(
                part.at[m, h, (x + k) % 4], part_in.at[m, h, x],
                p_send.at[m, h], p_recv.at[m, h], at_x(k),
            ).start()

    def combine(m, h):
        arrived(part_in.at[m, h], p_recv.at[m, h])
        total = part[m, h, x].astype(jnp.float32)
        for k in range(1, 4):
            total += part_in[m, h, (x + k) % 4].astype(jnp.float32)
        kv[m, h] = total.astype(jnp.bfloat16)

    scale = 1.0 / math.sqrt(HEAD_DIM)

    def spread(m, h, grad):
        dkv[m, h, x] = grad.astype(jnp.bfloat16)
        mine = dkv.at[m, h, x]
        for k in range(1, 4):
            remote(mine, mine, k_send.at[m, h], k_recv.at[m, h], at_x(k)).start()

    def queries(h):
        for j in range(4):
            wait_bytes(x_far.at[j, h], SHARD)
        total = jnp.zeros((ROWS, HEAD_DIM), jnp.float32)

        def add(k, total):
            at = pl.ds(pl.multiple_of(k * BLOCK, BLOCK), BLOCK)
            return total + jnp.dot(hid[:, at], wq[h, at, :], preferred_element_type=jnp.float32)

        qb[h] = lax.fori_loop(0, 4, add, total).astype(jnp.bfloat16)

    def soften(h):
        expo = jnp.exp(dot_nt(qb[h], kv[0, h]) * scale)
        soft = expo / jnp.sum(expo, axis=1, keepdims=True)
        probs[h] = soft
        head = hg[:, h * HEAD_DIM : (h + 1) * HEAD_DIM]
        spread(1, h, dot_tn(soft.astype(jnp.bfloat16), head))

    def attend(h):
        soft = probs[h]
        prob_grad = dot_nt(hg[:, h * HEAD_DIM : (h + 1) * HEAD_DIM], kv[1, h])
        mean = jnp.sum(prob_grad * soft, axis=1, keepdims=True)
        score_grad = (soft * (prob_grad - mean) * scale).astype(jnp.bfloat16)
        spread(0, h, dot_tn(score_grad, qb[h]))
        dq[h] = jnp.dot(score_grad, kv[0, h], preferred_element_type=jnp.float32).astype(
            jnp.bfloat16
        )

    def term(m, h, cols):
        left = dkv[m, h].reshape(4 * ROWS, HEAD_DIM)
        return dot_nt(left, wkv[m, h, cols, :])

    tiles = [slice(b * HEAD_DIM, (b + 1) * HEAD_DIM) for b in range(4)]

    def early_encoder():
        arrived(dkv.at[1, 0], k_recv.at[1, 0])
        arrived(dkv.at[1, 1], k_recv.at[1, 1])
        for at in tiles:
            de[:, at] = term(1, 0, at) + term(1, 1, at)

    def late_encoder():
        arrived(dkv.at[0, 0], k_recv.at[0, 0])
        for at in tiles:
            de[:, at] += term(0, 0, at)

    z_second(0)
    z_first(2)
    x_first(0, 1)
    x_first(0, 3)
    enc_x()
    norm()
    x_second(0, 0)
    x_second(1, 0)

    z_second(1)
    z_first(3)
    x_first(1, 1)
    x_first(1, 3)
    enc_y()
    wait_bytes(z_far.at[0], SHARD)
    x_first(0, 2)
    x_second(0, 1)
    x_second(0, 3)

    z_second(2)
    z_first(4)
    enc_core()
    wait_bytes(z_far.at[1], SHARD)
    x_first(1, 2)

    z_second(3)
    z_first(5)
    z_first(6)
    x_second(0, 2)
    x_second(1, 1)
    x_second(1, 3)
    x_second(1, 2)
    wait_for(enc.at[pl.ds(0, 256)], e_recv.at[3])
    share(0, 0)
    queries(0)
    queries(1)
    hg_load.wait()

    z_second(4)
    combine(0, 0)
    soften(0)

    z_second(5)
    share(0, 1)
    z_second(6)
    share(1, 0)
    combine(0, 1)
    soften(1)

    share(1, 1)
    combine(1, 0)
    attend(0)
    combine(1, 1)
    attend(1)

    def hidden_block(j):
        at = pl.ds(pl.multiple_of(j * BLOCK, BLOCK), BLOCK)
        low = (dot_nt(dq[0], wq[0, at, :]) + dot_nt(dq[1], wq[1, at, :])).astype(jnp.bfloat16)
        hp[j] = low
        product = low.astype(jnp.float32) * (xv[:, at].astype(jnp.float32) * inv[:, :1])
        gain = jnp.sum(product, axis=0, keepdims=True)
        product *= gain_ref[:, at]
        folded = product[:, :128]
        for b in range(8):
            note[j, pl.ds(8 + b, 1)] = gain[:, b * 128 : (b + 1) * 128]
            if b:
                folded += product[:, b * 128 : (b + 1) * 128]
        return folded

    edge = jnp.logical_or(t == 0, t == 3)
    inside = jnp.logical_not(edge)
    mate = t + 1 - 2 * (t % 2)
    outer = jnp.where(edge, 3 - t, 3 - mate)
    nearer = 3 - t + 3 - mate - outer

    def hand(block, slot, i, to):
        remote(
            block, hp_in.at[slot], h_send.at[i], h_recv.at[slot], (dp, pipe, to)
        ).start()

    folded = lax.fori_loop(
        0, 4, lambda j, folded: folded + hidden_block(j), jnp.zeros((ROWS, 128), jnp.float32)
    )

    note[:, pl.ds(0, 8), :] = jnp.broadcast_to(
        jnp.sum(folded.T, axis=0, keepdims=True)[None], (4, 8, 128)
    )
    for k in range(1, 4):
        remote(
            note.at[(t + k) % 4], note_in.at[t], i_send.at[0], i_recv.at[0], at_t(k)
        ).start()

    @pl.when(edge)
    def _():
        for i, j in enumerate((outer, nearer)):
            hand(hp.at[j], 2 + i, i, mate)

    early_encoder()
    late_encoder()
    arrived(note_in, i_recv.at[0])
    note_in[t] = note[t]
    noted = note_in[0] + note_in[1] + note_in[2] + note_in[3]
    mean = jnp.broadcast_to(noted[:1] / D, (128, 128)).T[:, :1]
    gz[z] = noted[8:]
    for k in range(1, 4):
        remote(gz.at[z], gz.at[z], g_send.at[0], g_recv.at[0], at_z(k)).start()

    hand(hp.at[mate], 0, 2, mate)

    arrived(dkv.at[0, 1], k_recv.at[0, 1])

    def seq_rows(s, k, c):
        return pl.ds(pl.multiple_of(s * ROWS + (k * 2 + c) * 16, 16), 16)

    halves = [slice(0, COLS), slice(COLS, 2 * COLS)]
    for b, cols in enumerate(halves):
        for lane in (cols.start, cols.start + HEAD_DIM):
            at = slice(lane, lane + HEAD_DIM)
            de[:, at] += term(0, 1, at)
        for s in range(4):
            for k in range(4):
                de1[b, k, s] = de[seq_rows(s, k, 1 - core), cols].astype(jnp.bfloat16)
        remote(de1.at[b], de1_in.at[b], d_send.at[0, b], d_recv.at[0, b], other_core).start()

    @pl.when(inside)
    def _():
        for i, j in enumerate((outer, nearer)):
            wait_for(hp_in.at[2 + i], h_recv.at[2 + i])
            both = hp[j].astype(jnp.float32) + hp_in[2 + i].astype(jnp.float32)
            hp_out[i] = both.astype(jnp.bfloat16)
            hand(hp_out.at[i], 1, i, j)

    for b, cols in enumerate(halves):
        wait_for(de1_in.at[b], d_recv.at[0, b])
        for k in range(1, 4):
            to = (y + k) % 4
            for s in range(4):
                de2[b, to, s] = (
                    de[seq_rows(s, to, core), cols] + de1_in[b, to, s].astype(jnp.float32)
                ).astype(jnp.bfloat16)
            remote(
                de2.at[b, to], de2_in.at[b, y], d_send.at[1, b], d_recv.at[1, b], at_y(k)
            ).start()

    quarters = [[] for _ in range(4)]
    for b, cols in enumerate(halves):
        arrived(de2_in.at[b], d_recv.at[1, b])
        for s in range(4):
            total = de[seq_rows(s, y, core), cols] + de1_in[b, y, s].astype(jnp.float32)
            for k in range(1, 4):
                total += de2_in[b, (y + k) % 4, s].astype(jnp.float32)
            low = total.astype(jnp.bfloat16)
            quarters[s] += [low[:, :HEAD_DIM], low[:, HEAD_DIM:]]
    stacked = jnp.concatenate([jnp.concatenate(q, axis=0) for q in quarters], axis=1)
    moved = regroup(stacked).astype(jnp.bfloat16)
    for s in range(4):
        for b in range(4):
            de3[s * 4 + b] = moved[b * 16 : (b + 1) * 16, s * HEAD_DIM : (s + 1) * HEAD_DIM]
    for k in range(1, 16):
        remote(
            de3.at[(x * 4 + t + k) % 16], de3_in.at[x * 4 + t],
            d_send.at[2, 0], d_recv.at[2, 0], at_plane(k),
        ).start()

    arrived(gz, g_recv.at[0])
    gx[x] = gz[0] + gz[1] + gz[2] + gz[3]
    for k in range(1, 4):
        remote(gx.at[x], gx.at[x], g_send.at[1], g_recv.at[1], at_x(k)).start()

    og_load.wait()
    at = pl.ds(pl.multiple_of(t * BLOCK, BLOCK), BLOCK)
    scale_col = inv[:, :1]
    normed = xv[:, at].astype(jnp.float32) * scale_col
    hidden_grad = hp[t].astype(jnp.float32)
    for k in range(2):
        wait_for(hp_in.at[k], h_recv.at[k])
        hidden_grad += hp_in[k].astype(jnp.float32)
    normed_grad = hidden_grad * gain_ref[:, at]
    ig_ref[0] = (
        og[...].astype(jnp.float32) + scale_col * (normed_grad - normed * mean)
    ).astype(jnp.bfloat16)

    arrived(gx, g_recv.at[1])
    gains = gx[0] + gx[1] + gx[2] + gx[3]
    for b in range(8):
        gg_ref[:, b * 128 : (b + 1) * 128] = gains[b : b + 1]

    wait_for(de3_in.at[pl.ds(0, 15)], d_recv.at[2, 0])
    de3_in[x * 4 + t] = de3[x * 4 + t]
    for b in range(4):
        summed = de3_in[b * 4].astype(jnp.float32)
        for k in range(1, 4):
            summed += de3_in[b * 4 + k].astype(jnp.float32)
        lines[:, b * HEAD_DIM : (b + 1) * HEAD_DIM] = summed
    for b in range(4):
        for k in range(4):
            eg_ref[:, b * BLOCK + k * HEAD_DIM : b * BLOCK + (k + 1) * HEAD_DIM] = lines[
                pl.ds(k * 4, 4), b * HEAD_DIM : (b + 1) * HEAD_DIM
            ]

    for c in range(len(PIECES)):
        wait_bytes(z_send.at[c], 3 * PIECES[c][3])
    for h in range(HEADS_HERE):
        wait_bytes(x_send.at[h], 12 * SHARD)
        for m in range(2):
            arrived(part.at[m, h], p_send.at[m, h])
            arrived(dkv.at[m, h], k_send.at[m, h])
    wait_for(enc64.at[pl.ds(0, 48)], e_send.at[0])
    wait_for(enc.at[pl.ds(0, 48)], e_send.at[1])
    wait_for(enc.at[pl.ds(0, 192)], e_send.at[2])
    wait_for(enc.at[pl.ds(0, 256)], e_send.at[3])
    for k in range(3):
        wait_for(hp.at[k], h_send.at[k])
    arrived(note, i_send.at[0])
    for b in range(2):
        wait_for(de1.at[b], d_send.at[0, b])
        arrived(de2.at[b], d_send.at[1, b])
    wait_for(de3.at[pl.ds(0, 15)], d_send.at[2, 0])
    arrived(gx, g_send.at[1])
    arrived(gz, g_send.at[0])


def shards(
    section_input, out_grad, head_grad, encoder, norm_gain, query_weight, key_weight, value_weight
):
    low, f32 = jnp.bfloat16, jnp.float32
    hbm = pl.BlockSpec(memory_space=pl.ANY)
    vmem = pl.BlockSpec(memory_space=pltpu.VMEM)
    dma = pltpu.SemaphoreType.DMA
    two = (2, HEADS_HERE)
    return pl.pallas_call(
        kernel,
        out_shape=(
            pltpu.VMEM((1, ROWS, BLOCK), low),
            pltpu.VMEM((4, D), f32),
            pltpu.VMEM((1, BLOCK), f32),
        ),
        in_specs=[hbm, hbm, hbm, vmem, vmem, hbm, hbm, hbm],
        out_specs=(vmem, vmem, vmem),
        scratch_shapes=[
            pltpu.VMEM((HEADS_HERE, D, HEAD_DIM), low),
            pltpu.VMEM(two + (BLOCK, HEAD_DIM), low),
            pltpu.VMEM((ROWS, D), low),
            pltpu.VMEM((ROWS, BLOCK), low),
            pltpu.VMEM((ROWS, COLS), low),
            pltpu.VMEM((16, BLOCK), f32),
            pltpu.VMEM((64, BLOCK), low),
            pltpu.VMEM((4, 16, BLOCK), low),
            pltpu.VMEM((4 * ROWS, BLOCK), low),
            pltpu.VMEM((ROWS, D), low),
            pltpu.VMEM((ROWS, 128), f32),
            pltpu.VMEM(two + (4, ROWS, HEAD_DIM), low),
            pltpu.VMEM(two + (4, ROWS, HEAD_DIM), low),
            pltpu.VMEM(two + (ROWS, HEAD_DIM), low),
            pltpu.VMEM((HEADS_HERE, ROWS, HEAD_DIM), low),
            pltpu.VMEM((HEADS_HERE, ROWS, ROWS), f32),
            pltpu.VMEM((HEADS_HERE, ROWS, HEAD_DIM), low),
            pltpu.VMEM(two + (4, ROWS, HEAD_DIM), low),
            pltpu.VMEM((4, ROWS, BLOCK), low),
            pltpu.VMEM((4, ROWS, BLOCK), low),
            pltpu.VMEM((2, ROWS, BLOCK), low),
            pltpu.VMEM((4, 16, 128), f32),
            pltpu.VMEM((4, 16, 128), f32),
            pltpu.VMEM((4 * ROWS, BLOCK), f32),
            pltpu.VMEM((2, 4, 4, 16, COLS), low),
            pltpu.VMEM((2, 4, 4, 16, COLS), low),
            pltpu.VMEM((2, 4, 4, 16, COLS), low),
            pltpu.VMEM((2, 4, 4, 16, COLS), low),
            pltpu.VMEM((16, 16, HEAD_DIM), low),
            pltpu.VMEM((16, 16, HEAD_DIM), low),
            pltpu.VMEM((4, 8, 128), f32),
            pltpu.VMEM((4, 8, 128), f32),
            dma((11,)),
            dma((len(PIECES),)),
            dma((HEADS_HERE,)),
            dma((len(PIECES),)),
            dma((len(PIECES),)),
            dma((4, HEADS_HERE)),
            dma((4, HEADS_HERE)),
            dma(two),
            dma(two),
            dma(two),
            dma(two),
            dma((4,)),
            dma((4,)),
            dma((3,)),
            dma((4,)),
            dma((1,)),
            dma((1,)),
            dma((3, 2)),
            dma((3, 2)),
            dma((2,)),
            dma((2,)),
        ],
        compiler_params=pltpu.CompilerParams(
            collective_id=0, has_side_effects=True, vmem_limit_bytes=60 * 1024 * 1024
        ),
        cost_estimate=pl.CostEstimate(
            flops=6 * 2 * ROWS * D * COLS, bytes_accessed=4 * 1024 * 1024, transcendentals=0
        ),
    )(
        section_input, out_grad, head_grad, encoder, norm_gain,
        query_weight, key_weight, value_weight,
    )


def solution(mesh):
    placed = (
        P("pipe", "dp", None),
        P("pipe", "dp", None),
        P("pipe", "dp", "tensor"),
        P(("dp", "pipe", "tensor"), None),
        P("pipe", None),
        P("pipe", "dp", "tensor"),
        P("pipe", "dp", "tensor"),
        P("pipe", "dp", "tensor"),
    )
    return jax.shard_map(
        shards,
        mesh=mesh,
        in_specs=placed,
        out_specs=(
            P("pipe", "dp", "tensor"),
            P(("dp", "pipe", "tensor"), None),
            P("pipe", "tensor"),
        ),
        check_vma=False,
    )
```

```python
import math

import jax
import jax.numpy as jnp
from jax import lax
from jax.experimental import pallas as pl
from jax.experimental.pallas import tpu as pltpu
from jax.sharding import PartitionSpec as P

HEAD_DIM = 256
HEADS_HERE = 2
COLS = 512
D = 4096
ROWS = 128
SHARD = 256
HALF = SHARD // 2
BLOCK = 1024
EPSILON = 1e-06
MESH = pl.DeviceIdType.MESH
QUARTER = SHARD // 4
PIECES = [
    (0, 0, 0, SHARD), (0, 1, 0, SHARD), (1, 0, 0, SHARD), (1, 1, 0, SHARD), (2, 0, 0, SHARD),
    (2, 1, 0, HALF), (2, 1, HALF, HALF),
]


def dot_nt(left, right):
    return lax.dot_general(
        left, right, (((1,), (1,)), ((), ())), preferred_element_type=jnp.float32
    )


def dot_tn(left, right):
    return lax.dot_general(
        left, right, (((0,), (0,)), ((), ())), preferred_element_type=jnp.float32
    )


def regroup(rows):
    i = lax.broadcasted_iota(jnp.int32, (64, 64), 0)
    j = lax.broadcasted_iota(jnp.int32, (64, 64), 1)
    source = (i % 16) // 4 * 16 + i // 16 * 4 + i % 4
    hot = jnp.where(j == source, 1.0, 0.0).astype(jnp.bfloat16)
    return jnp.dot(hot, rows, preferred_element_type=jnp.float32)


def kernel(
    x_hbm, og_hbm, hg_hbm, enc_ref, gain_hbm, wq_hbm, wk_hbm, wv_hbm,
    ig_ref, eg_ref, gg_ref,
    wq, wkv, xv, gain_ref, og, hg, lines, enc64, encx, enc, hid, inv, part, part_in, pg, pg_in, kh, qb, probs, dq, dkv,
    hp, hp_in, hp_out, note, note_in, de, de1, de1_in, de2, de2_in, de3, de3_in, gz, gx,
    local, z_send, x_send, z_near, z_far, x_near, x_far, p_send, p_recv, a_send, a_recv, k_send, k_recv,
    e_send, e_recv, h_send, h_recv, i_send, i_recv, d_send, d_recv, g_send, g_recv,
):
    dp = lax.axis_index("dp")
    pipe = lax.axis_index("pipe")
    t = lax.axis_index("tensor")
    x, z = dp // 4, dp % 4
    y, core = pipe // 2, pipe % 2

    def at_z(k):
        return (x * 4 + (z + k) % 4, pipe, t)

    def at_x(k):
        return ((x + k) % 4 * 4 + z, pipe, t)

    def at_y(k):
        return (dp, (y + k) % 4 * 2 + core, t)

    def at_t(k):
        return (dp, pipe, (t + k) % 4)

    def at_plane(k):
        to = (x * 4 + t + k) % 16
        return (to // 4 * 4 + z, pipe, to % 4)

    other_core = (dp, y * 2 + 1 - core, t)

    def remote(src, dst, send, recv, peer):
        return pltpu.make_async_remote_copy(
            src_ref=src, dst_ref=dst, send_sem=send, recv_sem=recv,
            device_id=peer, device_id_type=MESH,
        )

    def rows_of(ref, block, rows, start=0):
        return ref.at[pl.ds(pl.multiple_of(block * rows + start, 16), rows)]

    def wait_for(ref, sem):
        pltpu.make_async_copy(ref, ref, sem).wait()

    def arrived(ref, sem):
        wait_for(ref.at[pl.ds(0, 3)], sem)

    def piece(c, xx, zz, start=0, rows=None):
        m, h, first_row, count = PIECES[c]
        start, rows = start + first_row, rows or count
        if m == 0:
            first = (xx * 4 + zz) * SHARD + start
            return wq.at[h, pl.ds(pl.multiple_of(first, QUARTER), rows)]
        return wkv.at[m - 1, h, pl.ds(pl.multiple_of(zz * SHARD + start, QUARTER), rows)]

    sources = (wq_hbm, wk_hbm, wv_hbm)
    loads = [
        pltpu.make_async_copy(
            sources[m].at[0, pl.ds(start, rows), pl.ds(h * HEAD_DIM, HEAD_DIM)],
            piece(c, x, z), local.at[c],
        )
        for c, (m, h, start, rows) in enumerate(PIECES)
    ]
    x_load = pltpu.make_async_copy(x_hbm.at[0], xv, local.at[8])
    gain_load = pltpu.make_async_copy(gain_hbm, gain_ref, local.at[7])
    hg_load = pltpu.make_async_copy(hg_hbm.at[0], hg.at[x], local.at[9])
    og_load = pltpu.make_async_copy(
        og_hbm.at[0, :, pl.ds(pl.multiple_of(t * BLOCK, BLOCK), BLOCK)], og, local.at[10]
    )
    for copy in loads + [x_load, gain_load, hg_load, og_load]:
        copy.start()

    barrier = pltpu.get_barrier_semaphore()
    peers = [other_core]
    for k in range(1, 4):
        peers += [at_z(k), at_t(k), at_y(k)] + [((x + k) % 4 * 4 + z, pipe, b) for b in range(4)]
    for peer in peers:
        pl.semaphore_signal(barrier, inc=1, device_id=peer, device_id_type=MESH)
    for b in range(4):
        lines[pl.ds(b * 4, 4), :] = enc_ref[:, b * BLOCK : (b + 1) * BLOCK].astype(jnp.float32)
    enc64[pl.ds(pl.multiple_of(t * 16, 16), 16), :] = lines[...].astype(jnp.bfloat16)
    for copy in loads:
        copy.wait()
    pl.semaphore_wait(barrier, len(peers))

    def wait_bytes(sem, rows):
        wait_for(wq.at[0, pl.ds(0, rows)], sem)

    def z_first(c):
        own = piece(c, x, z)
        for k in (1, -1):
            remote(own, own, z_send.at[c], z_near.at[c], at_z(k)).start()

    def z_second(c):
        rows = PIECES[c][3]
        wait_bytes(z_near.at[c], 2 * rows)
        up = piece(c, x, (z + 3) % 4, rows // 2, rows // 2)
        remote(up, up, z_send.at[c], z_far.at[c], at_z(1)).start()
        down = piece(c, x, (z + 1) % 4, 0, rows // 2)
        remote(down, down, z_send.at[c], z_far.at[c], at_z(-1)).start()

    def x_first(h, j):
        own = piece(h, x, (z + j) % 4)
        for k in (1, -1):
            remote(own, own, x_send.at[h], x_near.at[j, h], at_x(k)).start()

    def x_second(h, j):
        wait_bytes(x_near.at[j, h], 2 * SHARD)
        up = piece(h, (x + 3) % 4, (z + j) % 4, HALF, HALF)
        remote(up, up, x_send.at[h], x_far.at[j, h], at_x(1)).start()
        down = piece(h, (x + 1) % 4, (z + j) % 4, 0, HALF)
        remote(down, down, x_send.at[h], x_far.at[j, h], at_x(-1)).start()

    own16 = rows_of(enc64, t, 16)
    for k in range(1, 4):
        remote(own16, own16, e_send.at[0], e_recv.at[0], at_t(k)).start()
    z_first(0)
    z_first(1)
    x_first(0, 0)
    x_first(1, 0)

    def enc_x():
        wait_for(enc64.at[pl.ds(0, 48)], e_recv.at[0])
        moved = regroup(enc64[...]).astype(jnp.bfloat16)
        for b in range(4):
            encx[b] = moved[b * 16 : (b + 1) * 16]
        enc[pl.ds(pl.multiple_of(pipe * 64 + x * 16, 16), 16), :] = encx[x]
        for k in range(1, 4):
            remote(
                encx.at[(x + k) % 4],
                enc.at[pl.ds(pl.multiple_of(pipe * 64 + x * 16, 16), 16)],
                e_send.at[1], e_recv.at[1], at_x(k),
            ).start()

    def enc_y():
        wait_for(enc.at[pl.ds(0, 48)], e_recv.at[1])
        mine = rows_of(enc, pipe, 64)
        for k in range(1, 4):
            remote(mine, mine, e_send.at[2], e_recv.at[2], at_y(k)).start()

    def enc_core():
        wait_for(enc.at[pl.ds(0, 192)], e_recv.at[2])
        for k in range(4):
            mine = rows_of(enc, k * 2 + core, 64)
            remote(mine, mine, e_send.at[3], e_recv.at[3], other_core).start()

    def norm():
        x_load.wait()
        gain_load.wait()
        total = jnp.zeros((ROWS, 1), jnp.float32)
        for b in range(4):
            block = xv[:, b * BLOCK : (b + 1) * BLOCK].astype(jnp.float32)
            total += jnp.sum(block * block, axis=1, keepdims=True)
        scale = lax.rsqrt(total / D + EPSILON)
        inv[...] = jnp.broadcast_to(scale, (ROWS, 128))
        for b in range(4):
            cols = slice(b * BLOCK, (b + 1) * BLOCK)
            normed = xv[:, cols].astype(jnp.float32) * scale
            hid[:, cols] = (normed * gain_ref[:, cols]).astype(jnp.bfloat16)

    def share(m, h):
        for c, (weight, head, _, rows) in enumerate(PIECES):
            if (weight, head) == (m + 1, h):
                wait_bytes(z_far.at[c], rows)
        rows = jnp.dot(enc[...], wkv[m, h], preferred_element_type=jnp.float32).astype(jnp.bfloat16)
        for p in range(8):
            for b in range(4):
                part[m, h, b, pl.ds(p * 16, 16), :] = rows[p * 64 + b * 16 : p * 64 + (b + 1) * 16]
        source, target = part.at[m, h], part_in.at[h]
        if m == 1:
            for b in range(4):
                head = hg[b, :, h * HEAD_DIM : (h + 1) * HEAD_DIM]
                pg[h, b] = dot_nt(head, part[m, h, b]).astype(jnp.bfloat16)
            source, target = pg.at[h], pg_in.at[h]
        for k in range(1, 4):
            remote(
                source.at[(x + k) % 4], target.at[x], p_send.at[m, h], p_recv.at[m, h], at_x(k)
            ).start()

    def combine(h):
        arrived(part_in.at[h], p_recv.at[0, h])
        total = part[0, h, x].astype(jnp.float32)
        for k in range(1, 4):
            total += part_in[h, (x + k) % 4].astype(jnp.float32)
        kh[h] = total.astype(jnp.bfloat16)

    scale = 1.0 / math.sqrt(HEAD_DIM)

    def spread(m, h, grad):
        dkv[m, h, x] = grad.astype(jnp.bfloat16)
        mine = dkv.at[m, h, x]
        for k in range(1, 4):
            remote(mine, mine, k_send.at[m, h], k_recv.at[m, h], at_x(k)).start()

    def queries(h):
        for j in range(4):
            wait_bytes(x_far.at[j, h], SHARD)
        total = jnp.zeros((ROWS, HEAD_DIM), jnp.float32)

        def add(k, total):
            at = pl.ds(pl.multiple_of(k * BLOCK, BLOCK), BLOCK)
            return total + jnp.dot(hid[:, at], wq[h, at, :], preferred_element_type=jnp.float32)

        qb[h] = lax.fori_loop(0, 4, add, total).astype(jnp.bfloat16)

    def soften(h):
        expo = jnp.exp(dot_nt(qb[h], kh[h]) * scale)
        soft = expo / jnp.sum(expo, axis=1, keepdims=True)
        probs[h] = soft
        head = hg[x, :, h * HEAD_DIM : (h + 1) * HEAD_DIM]
        spread(1, h, dot_tn(soft.astype(jnp.bfloat16), head))

    def attend(h):
        soft = probs[h]
        arrived(pg_in.at[h], p_recv.at[1, h])
        prob_grad = pg[h, x].astype(jnp.float32)
        for k in range(1, 4):
            prob_grad += pg_in[h, (x + k) % 4].astype(jnp.float32)
        mean = jnp.sum(prob_grad * soft, axis=1, keepdims=True)
        score_grad = (soft * (prob_grad - mean) * scale).astype(jnp.bfloat16)
        spread(0, h, dot_tn(score_grad, qb[h]))
        dq[h] = jnp.dot(score_grad, kh[h], preferred_element_type=jnp.float32).astype(
            jnp.bfloat16
        )

    def term(m, h, cols):
        left = dkv[m, h].reshape(4 * ROWS, HEAD_DIM)
        return dot_nt(left, wkv[m, h, cols, :])

    tiles = [slice(b * HEAD_DIM, (b + 1) * HEAD_DIM) for b in range(4)]

    def early_encoder():
        arrived(dkv.at[1, 0], k_recv.at[1, 0])
        arrived(dkv.at[1, 1], k_recv.at[1, 1])
        for at in tiles:
            de[:, at] = term(1, 0, at) + term(1, 1, at)

    def late_encoder():
        arrived(dkv.at[0, 0], k_recv.at[0, 0])
        for at in tiles:
            de[:, at] += term(0, 0, at)

    z_second(0)
    z_first(2)
    x_first(0, 1)
    x_first(0, 3)
    enc_x()
    norm()
    hg_load.wait()
    for k in range(1, 4):
        remote(hg.at[x], hg.at[x], a_send.at[0], a_recv.at[0], at_x(k)).start()
    x_second(0, 0)
    x_second(1, 0)

    z_second(1)
    z_first(3)
    x_first(1, 1)
    x_first(1, 3)
    enc_y()
    wait_bytes(z_far.at[0], SHARD)
    x_first(0, 2)
    x_second(0, 1)
    x_second(0, 3)

    z_second(2)
    z_first(4)
    enc_core()
    wait_bytes(z_far.at[1], SHARD)
    x_first(1, 2)

    z_second(3)
    z_first(5)
    z_first(6)
    x_second(0, 2)
    x_second(1, 1)
    x_second(1, 3)
    x_second(1, 2)
    wait_for(enc.at[pl.ds(0, 256)], e_recv.at[3])
    share(0, 0)
    queries(0)
    queries(1)
    arrived(hg, a_recv.at[0])

    z_second(4)
    combine(0)
    soften(0)

    z_second(5)
    share(0, 1)
    z_second(6)
    share(1, 0)
    combine(1)
    soften(1)

    share(1, 1)
    attend(0)
    attend(1)

    def hidden_block(j):
        at = pl.ds(pl.multiple_of(j * BLOCK, BLOCK), BLOCK)
        low = (dot_nt(dq[0], wq[0, at, :]) + dot_nt(dq[1], wq[1, at, :])).astype(jnp.bfloat16)
        hp[j] = low
        product = low.astype(jnp.float32) * (xv[:, at].astype(jnp.float32) * inv[:, :1])
        gain = jnp.sum(product, axis=0, keepdims=True)
        product *= gain_ref[:, at]
        folded = product[:, :128]
        for b in range(8):
            note[j, pl.ds(8 + b, 1)] = gain[:, b * 128 : (b + 1) * 128]
            if b:
                folded += product[:, b * 128 : (b + 1) * 128]
        return folded

    edge = jnp.logical_or(t == 0, t == 3)
    inside = jnp.logical_not(edge)
    mate = t + 1 - 2 * (t % 2)
    outer = jnp.where(edge, 3 - t, 3 - mate)
    nearer = 3 - t + 3 - mate - outer

    def hand(block, slot, i, to):
        remote(
            block, hp_in.at[slot], h_send.at[i], h_recv.at[slot], (dp, pipe, to)
        ).start()

    folded = lax.fori_loop(
        0, 4, lambda j, folded: folded + hidden_block(j), jnp.zeros((ROWS, 128), jnp.float32)
    )

    note[:, pl.ds(0, 8), :] = jnp.broadcast_to(
        jnp.sum(folded.T, axis=0, keepdims=True)[None], (4, 8, 128)
    )
    for k in range(1, 4):
        remote(
            note.at[(t + k) % 4], note_in.at[t], i_send.at[0], i_recv.at[0], at_t(k)
        ).start()

    @pl.when(edge)
    def _():
        for i, j in enumerate((outer, nearer)):
            hand(hp.at[j], 2 + i, i, mate)

    early_encoder()
    late_encoder()
    arrived(note_in, i_recv.at[0])
    note_in[t] = note[t]
    noted = note_in[0] + note_in[1] + note_in[2] + note_in[3]
    mean = jnp.broadcast_to(noted[:1] / D, (128, 128)).T[:, :1]
    gz[z] = noted[8:]
    for k in range(1, 4):
        remote(gz.at[z], gz.at[z], g_send.at[0], g_recv.at[0], at_z(k)).start()

    hand(hp.at[mate], 0, 2, mate)

    arrived(dkv.at[0, 1], k_recv.at[0, 1])

    def seq_rows(s, k, c):
        return pl.ds(pl.multiple_of(s * ROWS + (k * 2 + c) * 16, 16), 16)

    halves = [slice(0, COLS), slice(COLS, 2 * COLS)]
    for b, cols in enumerate(halves):
        for lane in (cols.start, cols.start + HEAD_DIM):
            at = slice(lane, lane + HEAD_DIM)
            de[:, at] += term(0, 1, at)
        for s in range(4):
            for k in range(4):
                de1[b, k, s] = de[seq_rows(s, k, 1 - core), cols].astype(jnp.bfloat16)
        remote(de1.at[b], de1_in.at[b], d_send.at[0, b], d_recv.at[0, b], other_core).start()

    @pl.when(inside)
    def _():
        for i, j in enumerate((outer, nearer)):
            wait_for(hp_in.at[2 + i], h_recv.at[2 + i])
            both = hp[j].astype(jnp.float32) + hp_in[2 + i].astype(jnp.float32)
            hp_out[i] = both.astype(jnp.bfloat16)
            hand(hp_out.at[i], 1, i, j)

    for b, cols in enumerate(halves):
        wait_for(de1_in.at[b], d_recv.at[0, b])
        for k in range(1, 4):
            to = (y + k) % 4
            for s in range(4):
                de2[b, to, s] = (
                    de[seq_rows(s, to, core), cols] + de1_in[b, to, s].astype(jnp.float32)
                ).astype(jnp.bfloat16)
            remote(
                de2.at[b, to], de2_in.at[b, y], d_send.at[1, b], d_recv.at[1, b], at_y(k)
            ).start()

    quarters = [[] for _ in range(4)]
    for b, cols in enumerate(halves):
        arrived(de2_in.at[b], d_recv.at[1, b])
        for s in range(4):
            total = de[seq_rows(s, y, core), cols] + de1_in[b, y, s].astype(jnp.float32)
            for k in range(1, 4):
                total += de2_in[b, (y + k) % 4, s].astype(jnp.float32)
            low = total.astype(jnp.bfloat16)
            quarters[s] += [low[:, :HEAD_DIM], low[:, HEAD_DIM:]]
    stacked = jnp.concatenate([jnp.concatenate(q, axis=0) for q in quarters], axis=1)
    moved = regroup(stacked).astype(jnp.bfloat16)
    for s in range(4):
        for b in range(4):
            de3[s * 4 + b] = moved[b * 16 : (b + 1) * 16, s * HEAD_DIM : (s + 1) * HEAD_DIM]
    for k in range(1, 16):
        remote(
            de3.at[(x * 4 + t + k) % 16], de3_in.at[x * 4 + t],
            d_send.at[2, 0], d_recv.at[2, 0], at_plane(k),
        ).start()

    arrived(gz, g_recv.at[0])
    gx[x] = gz[0] + gz[1] + gz[2] + gz[3]
    for k in range(1, 4):
        remote(gx.at[x], gx.at[x], g_send.at[1], g_recv.at[1], at_x(k)).start()

    og_load.wait()
    at = pl.ds(pl.multiple_of(t * BLOCK, BLOCK), BLOCK)
    scale_col = inv[:, :1]
    normed = xv[:, at].astype(jnp.float32) * scale_col
    hidden_grad = hp[t].astype(jnp.float32)
    for k in range(2):
        wait_for(hp_in.at[k], h_recv.at[k])
        hidden_grad += hp_in[k].astype(jnp.float32)
    normed_grad = hidden_grad * gain_ref[:, at]
    ig_ref[0] = (
        og[...].astype(jnp.float32) + scale_col * (normed_grad - normed * mean)
    ).astype(jnp.bfloat16)

    arrived(gx, g_recv.at[1])
    gains = gx[0] + gx[1] + gx[2] + gx[3]
    for b in range(8):
        gg_ref[:, b * 128 : (b + 1) * 128] = gains[b : b + 1]

    wait_for(de3_in.at[pl.ds(0, 15)], d_recv.at[2, 0])
    de3_in[x * 4 + t] = de3[x * 4 + t]
    for b in range(4):
        summed = de3_in[b * 4].astype(jnp.float32)
        for k in range(1, 4):
            summed += de3_in[b * 4 + k].astype(jnp.float32)
        lines[:, b * HEAD_DIM : (b + 1) * HEAD_DIM] = summed
    for b in range(4):
        for k in range(4):
            eg_ref[:, b * BLOCK + k * HEAD_DIM : b * BLOCK + (k + 1) * HEAD_DIM] = lines[
                pl.ds(k * 4, 4), b * HEAD_DIM : (b + 1) * HEAD_DIM
            ]

    for c in range(len(PIECES)):
        wait_bytes(z_send.at[c], 3 * PIECES[c][3])
    for h in range(HEADS_HERE):
        wait_bytes(x_send.at[h], 12 * SHARD)
        for m in range(2):
            arrived((part.at[0, h], pg.at[h])[m], p_send.at[m, h])
            arrived(dkv.at[m, h], k_send.at[m, h])
    arrived(hg, a_send.at[0])
    wait_for(enc64.at[pl.ds(0, 48)], e_send.at[0])
    wait_for(enc.at[pl.ds(0, 48)], e_send.at[1])
    wait_for(enc.at[pl.ds(0, 192)], e_send.at[2])
    wait_for(enc.at[pl.ds(0, 256)], e_send.at[3])
    for k in range(3):
        wait_for(hp.at[k], h_send.at[k])
    arrived(note, i_send.at[0])
    for b in range(2):
        wait_for(de1.at[b], d_send.at[0, b])
        arrived(de2.at[b], d_send.at[1, b])
    wait_for(de3.at[pl.ds(0, 15)], d_send.at[2, 0])
    arrived(gx, g_send.at[1])
    arrived(gz, g_send.at[0])


def shards(
    section_input, out_grad, head_grad, encoder, norm_gain, query_weight, key_weight, value_weight
):
    low, f32 = jnp.bfloat16, jnp.float32
    hbm = pl.BlockSpec(memory_space=pl.ANY)
    vmem = pl.BlockSpec(memory_space=pltpu.VMEM)
    dma = pltpu.SemaphoreType.DMA
    two = (2, HEADS_HERE)
    return pl.pallas_call(
        kernel,
        out_shape=(
            pltpu.VMEM((1, ROWS, BLOCK), low),
            pltpu.VMEM((4, D), f32),
            pltpu.VMEM((1, BLOCK), f32),
        ),
        in_specs=[hbm, hbm, hbm, vmem, hbm, hbm, hbm, hbm],
        out_specs=(vmem, vmem, vmem),
        scratch_shapes=[
            pltpu.VMEM((HEADS_HERE, D, HEAD_DIM), low),
            pltpu.VMEM(two + (BLOCK, HEAD_DIM), low),
            pltpu.VMEM((ROWS, D), low),
            pltpu.VMEM((1, D), f32),
            pltpu.VMEM((ROWS, BLOCK), low),
            pltpu.VMEM((4, ROWS, COLS), low),
            pltpu.VMEM((16, BLOCK), f32),
            pltpu.VMEM((64, BLOCK), low),
            pltpu.VMEM((4, 16, BLOCK), low),
            pltpu.VMEM((4 * ROWS, BLOCK), low),
            pltpu.VMEM((ROWS, D), low),
            pltpu.VMEM((ROWS, 128), f32),
            pltpu.VMEM(two + (4, ROWS, HEAD_DIM), low),
            pltpu.VMEM((HEADS_HERE, 4, ROWS, HEAD_DIM), low),
            pltpu.VMEM((HEADS_HERE, 4, ROWS, ROWS), low),
            pltpu.VMEM((HEADS_HERE, 4, ROWS, ROWS), low),
            pltpu.VMEM((HEADS_HERE, ROWS, HEAD_DIM), low),
            pltpu.VMEM((HEADS_HERE, ROWS, HEAD_DIM), low),
            pltpu.VMEM((HEADS_HERE, ROWS, ROWS), f32),
            pltpu.VMEM((HEADS_HERE, ROWS, HEAD_DIM), low),
            pltpu.VMEM(two + (4, ROWS, HEAD_DIM), low),
            pltpu.VMEM((4, ROWS, BLOCK), low),
            pltpu.VMEM((4, ROWS, BLOCK), low),
            pltpu.VMEM((2, ROWS, BLOCK), low),
            pltpu.VMEM((4, 16, 128), f32),
            pltpu.VMEM((4, 16, 128), f32),
            pltpu.VMEM((4 * ROWS, BLOCK), f32),
            pltpu.VMEM((2, 4, 4, 16, COLS), low),
            pltpu.VMEM((2, 4, 4, 16, COLS), low),
            pltpu.VMEM((2, 4, 4, 16, COLS), low),
            pltpu.VMEM((2, 4, 4, 16, COLS), low),
            pltpu.VMEM((16, 16, HEAD_DIM), low),
            pltpu.VMEM((16, 16, HEAD_DIM), low),
            pltpu.VMEM((4, 8, 128), f32),
            pltpu.VMEM((4, 8, 128), f32),
            dma((11,)),
            dma((len(PIECES),)),
            dma((HEADS_HERE,)),
            dma((len(PIECES),)),
            dma((len(PIECES),)),
            dma((4, HEADS_HERE)),
            dma((4, HEADS_HERE)),
            dma(two),
            dma(two),
            dma((1,)),
            dma((1,)),
            dma(two),
            dma(two),
            dma((4,)),
            dma((4,)),
            dma((3,)),
            dma((4,)),
            dma((1,)),
            dma((1,)),
            dma((3, 2)),
            dma((3, 2)),
            dma((2,)),
            dma((2,)),
        ],
        compiler_params=pltpu.CompilerParams(
            collective_id=0, has_side_effects=True, vmem_limit_bytes=60 * 1024 * 1024
        ),
        cost_estimate=pl.CostEstimate(
            flops=6 * 2 * ROWS * D * COLS, bytes_accessed=4 * 1024 * 1024, transcendentals=0
        ),
    )(
        section_input, out_grad, head_grad, encoder, norm_gain,
        query_weight, key_weight, value_weight,
    )


def solution(mesh):
    placed = (
        P("pipe", "dp", None),
        P("pipe", "dp", None),
        P("pipe", "dp", "tensor"),
        P(("dp", "pipe", "tensor"), None),
        P("pipe", None),
        P("pipe", "dp", "tensor"),
        P("pipe", "dp", "tensor"),
        P("pipe", "dp", "tensor"),
    )
    return jax.shard_map(
        shards,
        mesh=mesh,
        in_specs=placed,
        out_specs=(
            P("pipe", "dp", "tensor"),
            P(("dp", "pipe", "tensor"), None),
            P("pipe", "tensor"),
        ),
        check_vma=False,
    )
```

```python
import math

import jax
import jax.numpy as jnp
from jax import lax
from jax.experimental import pallas as pl
from jax.experimental.pallas import tpu as pltpu
from jax.sharding import PartitionSpec as P

HEAD_DIM = 256
HEADS_HERE = 2
COLS = 512
D = 4096
ROWS = 128
SHARD = 256
HALF = SHARD // 2
BLOCK = 1024
EPSILON = 1e-06
MESH = pl.DeviceIdType.MESH
QUARTER = SHARD // 4
PIECES = [
    (0, 0, 0, SHARD), (0, 1, 0, SHARD), (1, 0, 0, SHARD), (1, 1, 0, SHARD), (2, 0, 0, SHARD),
    (2, 1, 0, HALF), (2, 1, HALF, HALF),
]


def dot_nt(left, right):
    return lax.dot_general(
        left, right, (((1,), (1,)), ((), ())), preferred_element_type=jnp.float32
    )


def dot_tn(left, right):
    return lax.dot_general(
        left, right, (((0,), (0,)), ((), ())), preferred_element_type=jnp.float32
    )


def regroup(rows):
    i = lax.broadcasted_iota(jnp.int32, (64, 64), 0)
    j = lax.broadcasted_iota(jnp.int32, (64, 64), 1)
    source = (i % 16) // 4 * 16 + i // 16 * 4 + i % 4
    hot = jnp.where(j == source, 1.0, 0.0).astype(jnp.bfloat16)
    return jnp.dot(hot, rows, preferred_element_type=jnp.float32)


def kernel(
    x_hbm, og_hbm, hg_hbm, enc_ref, gain_hbm, wq_hbm, wk_hbm, wv_hbm,
    ig_ref, eg_ref, gg_ref,
    wq, wkv, xv, gain_ref, og, hg, lines, enc64, encx, enc, hid, inv, part, part_in, pg, pg_in, kh, qb, probs, dq, dkv,
    hp, hp_in, hp_out, note, note_in, de, de1, de1_in, de2, de2_in, de3, de3_in, gz, gx,
    local, z_send, x_send, z_near, z_far, x_near, x_far, p_send, p_recv, a_send, a_recv, k_send, k_recv,
    e_send, e_recv, h_send, h_recv, i_send, i_recv, d_send, d_recv, g_send, g_recv,
):
    dp = lax.axis_index("dp")
    pipe = lax.axis_index("pipe")
    t = lax.axis_index("tensor")
    x, z = dp // 4, dp % 4
    y, core = pipe // 2, pipe % 2

    def at_z(k):
        return (x * 4 + (z + k) % 4, pipe, t)

    def at_x(k):
        return ((x + k) % 4 * 4 + z, pipe, t)

    def at_y(k):
        return (dp, (y + k) % 4 * 2 + core, t)

    def at_t(k):
        return (dp, pipe, (t + k) % 4)

    def at_plane(k):
        to = (x * 4 + t + k) % 16
        return (to // 4 * 4 + z, pipe, to % 4)

    other_core = (dp, y * 2 + 1 - core, t)

    def remote(src, dst, send, recv, peer):
        return pltpu.make_async_remote_copy(
            src_ref=src, dst_ref=dst, send_sem=send, recv_sem=recv,
            device_id=peer, device_id_type=MESH,
        )

    def rows_of(ref, block, rows, start=0):
        return ref.at[pl.ds(pl.multiple_of(block * rows + start, 16), rows)]

    def wait_for(ref, sem):
        pltpu.make_async_copy(ref, ref, sem).wait()

    def arrived(ref, sem):
        wait_for(ref.at[pl.ds(0, 3)], sem)

    def piece(c, xx, zz, start=0, rows=None):
        m, h, first_row, count = PIECES[c]
        start, rows = start + first_row, rows or count
        if m == 0:
            first = (xx * 4 + zz) * SHARD + start
            return wq.at[h, pl.ds(pl.multiple_of(first, QUARTER), rows)]
        return wkv.at[m - 1, h, pl.ds(pl.multiple_of(zz * SHARD + start, QUARTER), rows)]

    sources = (wq_hbm, wk_hbm, wv_hbm)
    loads = [
        pltpu.make_async_copy(
            sources[m].at[0, pl.ds(start, rows), pl.ds(h * HEAD_DIM, HEAD_DIM)],
            piece(c, x, z), local.at[c],
        )
        for c, (m, h, start, rows) in enumerate(PIECES)
    ]
    x_load = pltpu.make_async_copy(x_hbm.at[0], xv, local.at[8])
    gain_load = pltpu.make_async_copy(gain_hbm, gain_ref, local.at[7])
    hg_load = pltpu.make_async_copy(hg_hbm.at[0], hg.at[x], local.at[9])
    og_load = pltpu.make_async_copy(
        og_hbm.at[0, :, pl.ds(pl.multiple_of(t * BLOCK, BLOCK), BLOCK)], og, local.at[10]
    )
    for copy in loads + [x_load, gain_load, hg_load, og_load]:
        copy.start()

    barrier = pltpu.get_barrier_semaphore()
    peers = [other_core]
    for k in range(1, 4):
        peers += [at_z(k), at_t(k), at_y(k)] + [((x + k) % 4 * 4 + z, pipe, b) for b in range(4)]
    for peer in peers:
        pl.semaphore_signal(barrier, inc=1, device_id=peer, device_id_type=MESH)
    for b in range(4):
        lines[pl.ds(b * 4, 4), :] = enc_ref[:, b * BLOCK : (b + 1) * BLOCK].astype(jnp.float32)
    enc64[pl.ds(pl.multiple_of(t * 16, 16), 16), :] = lines[...].astype(jnp.bfloat16)
    for copy in loads:
        copy.wait()
    pl.semaphore_wait(barrier, len(peers))

    def wait_bytes(sem, rows):
        wait_for(wq.at[0, pl.ds(0, rows)], sem)

    def z_first(c):
        own = piece(c, x, z)
        for k in (1, -1):
            remote(own, own, z_send.at[c], z_near.at[c], at_z(k)).start()

    def z_second(c):
        rows = PIECES[c][3]
        wait_bytes(z_near.at[c], 2 * rows)
        up = piece(c, x, (z + 3) % 4, rows // 2, rows // 2)
        remote(up, up, z_send.at[c], z_far.at[c], at_z(1)).start()
        down = piece(c, x, (z + 1) % 4, 0, rows // 2)
        remote(down, down, z_send.at[c], z_far.at[c], at_z(-1)).start()

    def x_first(h, j):
        own = piece(h, x, (z + j) % 4)
        for k in (1, -1):
            remote(own, own, x_send.at[h], x_near.at[j, h], at_x(k)).start()

    def x_second(h, j):
        wait_bytes(x_near.at[j, h], 2 * SHARD)
        up = piece(h, (x + 3) % 4, (z + j) % 4, HALF, HALF)
        remote(up, up, x_send.at[h], x_far.at[j, h], at_x(1)).start()
        down = piece(h, (x + 1) % 4, (z + j) % 4, 0, HALF)
        remote(down, down, x_send.at[h], x_far.at[j, h], at_x(-1)).start()

    own16 = rows_of(enc64, t, 16)
    for k in range(1, 4):
        remote(own16, own16, e_send.at[0], e_recv.at[0], at_t(k)).start()
    z_first(0)
    z_first(1)
    x_first(0, 0)
    x_first(1, 0)

    def enc_x():
        wait_for(enc64.at[pl.ds(0, 48)], e_recv.at[0])
        moved = regroup(enc64[...]).astype(jnp.bfloat16)
        for b in range(4):
            encx[b] = moved[b * 16 : (b + 1) * 16]
        enc[pl.ds(pl.multiple_of(pipe * 64 + x * 16, 16), 16), :] = encx[x]
        for k in range(1, 4):
            remote(
                encx.at[(x + k) % 4],
                enc.at[pl.ds(pl.multiple_of(pipe * 64 + x * 16, 16), 16)],
                e_send.at[1], e_recv.at[1], at_x(k),
            ).start()

    def enc_y():
        wait_for(enc.at[pl.ds(0, 48)], e_recv.at[1])
        mine = rows_of(enc, pipe, 64)
        for k in range(1, 4):
            remote(mine, mine, e_send.at[2], e_recv.at[2], at_y(k)).start()

    def enc_core():
        wait_for(enc.at[pl.ds(0, 192)], e_recv.at[2])
        for k in range(4):
            mine = rows_of(enc, k * 2 + core, 64)
            remote(mine, mine, e_send.at[3], e_recv.at[3], other_core).start()

    def norm():
        x_load.wait()
        gain_load.wait()
        total = jnp.zeros((ROWS, 1), jnp.float32)
        for b in range(4):
            block = xv[:, b * BLOCK : (b + 1) * BLOCK].astype(jnp.float32)
            total += jnp.sum(block * block, axis=1, keepdims=True)
        scale = lax.rsqrt(total / D + EPSILON)
        inv[...] = jnp.broadcast_to(scale, (ROWS, 128))
        for b in range(4):
            cols = slice(b * BLOCK, (b + 1) * BLOCK)
            normed = xv[:, cols].astype(jnp.float32) * scale
            hid[:, cols] = (normed * gain_ref[:, cols]).astype(jnp.bfloat16)

    def share(m, h):
        for c, (weight, head, _, rows) in enumerate(PIECES):
            if (weight, head) == (m + 1, h):
                wait_bytes(z_far.at[c], rows)
        rows = jnp.dot(enc[...], wkv[m, h], preferred_element_type=jnp.float32).astype(jnp.bfloat16)
        for p in range(8):
            for b in range(4):
                part[m, h, b, pl.ds(p * 16, 16), :] = rows[p * 64 + b * 16 : p * 64 + (b + 1) * 16]
        source, target = part.at[m, h], part_in.at[h]
        if m == 1:
            for b in range(4):
                head = hg[b, :, h * HEAD_DIM : (h + 1) * HEAD_DIM]
                pg[h, b] = dot_nt(head, part[m, h, b]).astype(jnp.bfloat16)
            source, target = pg.at[h], pg_in.at[h]
        for k in range(1, 4):
            remote(
                source.at[(x + k) % 4], target.at[x], p_send.at[m, h], p_recv.at[m, h], at_x(k)
            ).start()

    def combine(h):
        arrived(part_in.at[h], p_recv.at[0, h])
        total = part[0, h, x].astype(jnp.float32)
        for k in range(1, 4):
            total += part_in[h, (x + k) % 4].astype(jnp.float32)
        kh[h] = total.astype(jnp.bfloat16)

    scale = 1.0 / math.sqrt(HEAD_DIM)

    def spread(m, h, grad):
        dkv[m, h, x] = grad.astype(jnp.bfloat16)
        mine = dkv.at[m, h, x]
        for k in range(1, 4):
            remote(mine, mine, k_send.at[m, h], k_recv.at[m, h], at_x(k)).start()

    def queries(h):
        for j in range(4):
            wait_bytes(x_far.at[j, h], SHARD)
        total = jnp.zeros((ROWS, HEAD_DIM), jnp.float32)

        def add(k, total):
            at = pl.ds(pl.multiple_of(k * BLOCK, BLOCK), BLOCK)
            return total + jnp.dot(hid[:, at], wq[h, at, :], preferred_element_type=jnp.float32)

        qb[h] = lax.fori_loop(0, 4, add, total).astype(jnp.bfloat16)

    def soften(h):
        expo = jnp.exp(dot_nt(qb[h], kh[h]) * scale)
        soft = expo / jnp.sum(expo, axis=1, keepdims=True)
        probs[h] = soft
        head = hg[x, :, h * HEAD_DIM : (h + 1) * HEAD_DIM]
        spread(1, h, dot_tn(soft.astype(jnp.bfloat16), head))

    def attend(h):
        soft = probs[h]
        arrived(pg_in.at[h], p_recv.at[1, h])
        prob_grad = pg[h, x].astype(jnp.float32)
        for k in range(1, 4):
            prob_grad += pg_in[h, (x + k) % 4].astype(jnp.float32)
        mean = jnp.sum(prob_grad * soft, axis=1, keepdims=True)
        score_grad = (soft * (prob_grad - mean) * scale).astype(jnp.bfloat16)
        spread(0, h, dot_tn(score_grad, qb[h]))
        dq[h] = jnp.dot(score_grad, kh[h], preferred_element_type=jnp.float32).astype(
            jnp.bfloat16
        )

    def term(m, h, cols):
        left = dkv[m, h].reshape(4 * ROWS, HEAD_DIM)
        return dot_nt(left, wkv[m, h, cols, :])

    tiles = [slice(b * HEAD_DIM, (b + 1) * HEAD_DIM) for b in range(4)]

    def early_encoder():
        arrived(dkv.at[1, 0], k_recv.at[1, 0])
        arrived(dkv.at[1, 1], k_recv.at[1, 1])
        for at in tiles:
            de[:, at] = term(1, 0, at) + term(1, 1, at)

    def late_encoder():
        arrived(dkv.at[0, 0], k_recv.at[0, 0])
        for at in tiles:
            de[:, at] += term(0, 0, at)

    z_second(0)
    z_first(2)
    x_first(0, 1)
    x_first(0, 3)
    enc_x()
    norm()
    hg_load.wait()
    for k in range(1, 4):
        remote(hg.at[x], hg.at[x], a_send.at[0], a_recv.at[0], at_x(k)).start()
    x_second(0, 0)
    x_second(1, 0)

    z_second(1)
    z_first(3)
    x_first(1, 1)
    x_first(1, 3)
    enc_y()
    wait_bytes(z_far.at[0], SHARD)
    x_first(0, 2)
    x_second(0, 1)
    x_second(0, 3)

    z_second(2)
    z_first(4)
    enc_core()
    wait_bytes(z_far.at[1], SHARD)
    x_first(1, 2)

    z_second(3)
    z_first(5)
    z_first(6)
    x_second(0, 2)
    x_second(1, 1)
    x_second(1, 3)
    x_second(1, 2)
    wait_for(enc.at[pl.ds(0, 256)], e_recv.at[3])
    queries(0)
    queries(1)
    arrived(hg, a_recv.at[0])

    z_second(4)
    share(0, 0)

    z_second(5)
    share(0, 1)
    combine(0)
    soften(0)
    z_second(6)
    share(1, 0)
    combine(1)
    soften(1)

    share(1, 1)
    attend(0)
    attend(1)

    def hidden_block(j):
        at = pl.ds(pl.multiple_of(j * BLOCK, BLOCK), BLOCK)
        low = (dot_nt(dq[0], wq[0, at, :]) + dot_nt(dq[1], wq[1, at, :])).astype(jnp.bfloat16)
        hp[j] = low
        product = low.astype(jnp.float32) * (xv[:, at].astype(jnp.float32) * inv[:, :1])
        gain = jnp.sum(product, axis=0, keepdims=True)
        product *= gain_ref[:, at]
        folded = product[:, :128]
        for b in range(8):
            note[j, pl.ds(8 + b, 1)] = gain[:, b * 128 : (b + 1) * 128]
            if b:
                folded += product[:, b * 128 : (b + 1) * 128]
        return folded

    edge = jnp.logical_or(t == 0, t == 3)
    inside = jnp.logical_not(edge)
    mate = t + 1 - 2 * (t % 2)
    outer = jnp.where(edge, 3 - t, 3 - mate)
    nearer = 3 - t + 3 - mate - outer

    def hand(block, slot, i, to):
        remote(
            block, hp_in.at[slot], h_send.at[i], h_recv.at[slot], (dp, pipe, to)
        ).start()

    folded = lax.fori_loop(
        0, 4, lambda j, folded: folded + hidden_block(j), jnp.zeros((ROWS, 128), jnp.float32)
    )

    note[:, pl.ds(0, 8), :] = jnp.broadcast_to(
        jnp.sum(folded.T, axis=0, keepdims=True)[None], (4, 8, 128)
    )
    for k in range(1, 4):
        remote(
            note.at[(t + k) % 4], note_in.at[t], i_send.at[0], i_recv.at[0], at_t(k)
        ).start()

    @pl.when(edge)
    def _():
        for i, j in enumerate((outer, nearer)):
            hand(hp.at[j], 2 + i, i, mate)

    early_encoder()
    late_encoder()
    arrived(note_in, i_recv.at[0])
    note_in[t] = note[t]
    noted = note_in[0] + note_in[1] + note_in[2] + note_in[3]
    mean = jnp.broadcast_to(noted[:1] / D, (128, 128)).T[:, :1]
    gz[z] = noted[8:]
    for k in range(1, 4):
        remote(gz.at[z], gz.at[z], g_send.at[0], g_recv.at[0], at_z(k)).start()

    hand(hp.at[mate], 0, 2, mate)

    arrived(dkv.at[0, 1], k_recv.at[0, 1])

    def seq_rows(s, k, c):
        return pl.ds(pl.multiple_of(s * ROWS + (k * 2 + c) * 16, 16), 16)

    halves = [slice(0, COLS), slice(COLS, 2 * COLS)]
    for b, cols in enumerate(halves):
        for lane in (cols.start, cols.start + HEAD_DIM):
            at = slice(lane, lane + HEAD_DIM)
            de[:, at] += term(0, 1, at)
        for s in range(4):
            for k in range(4):
                de1[b, k, s] = de[seq_rows(s, k, 1 - core), cols].astype(jnp.bfloat16)
        remote(de1.at[b], de1_in.at[b], d_send.at[0, b], d_recv.at[0, b], other_core).start()

    @pl.when(inside)
    def _():
        for i, j in enumerate((outer, nearer)):
            wait_for(hp_in.at[2 + i], h_recv.at[2 + i])
            both = hp[j].astype(jnp.float32) + hp_in[2 + i].astype(jnp.float32)
            hp_out[i] = both.astype(jnp.bfloat16)
            hand(hp_out.at[i], 1, i, j)

    for b, cols in enumerate(halves):
        wait_for(de1_in.at[b], d_recv.at[0, b])
        for k in (2, 1, 3):
            to = (y + k) % 4
            for s in range(4):
                de2[b, to, s] = (
                    de[seq_rows(s, to, core), cols] + de1_in[b, to, s].astype(jnp.float32)
                ).astype(jnp.bfloat16)
            remote(
                de2.at[b, to], de2_in.at[b, y], d_send.at[1, b], d_recv.at[1, b], at_y(k)
            ).start()

    quarters = [[] for _ in range(4)]
    for b, cols in enumerate(halves):
        arrived(de2_in.at[b], d_recv.at[1, b])
        for s in range(4):
            total = de[seq_rows(s, y, core), cols] + de1_in[b, y, s].astype(jnp.float32)
            for k in range(1, 4):
                total += de2_in[b, (y + k) % 4, s].astype(jnp.float32)
            low = total.astype(jnp.bfloat16)
            quarters[s] += [low[:, :HEAD_DIM], low[:, HEAD_DIM:]]
    stacked = jnp.concatenate([jnp.concatenate(q, axis=0) for q in quarters], axis=1)
    moved = regroup(stacked).astype(jnp.bfloat16)
    for s in range(4):
        for b in range(4):
            de3[s * 4 + b] = moved[b * 16 : (b + 1) * 16, s * HEAD_DIM : (s + 1) * HEAD_DIM]
    for k in range(1, 16):
        remote(
            de3.at[(x * 4 + t + k) % 16], de3_in.at[x * 4 + t],
            d_send.at[2, 0], d_recv.at[2, 0], at_plane(k),
        ).start()

    arrived(gz, g_recv.at[0])
    gx[x] = gz[0] + gz[1] + gz[2] + gz[3]
    for k in range(1, 4):
        remote(gx.at[x], gx.at[x], g_send.at[1], g_recv.at[1], at_x(k)).start()

    og_load.wait()
    at = pl.ds(pl.multiple_of(t * BLOCK, BLOCK), BLOCK)
    scale_col = inv[:, :1]
    normed = xv[:, at].astype(jnp.float32) * scale_col
    hidden_grad = hp[t].astype(jnp.float32)
    for k in range(2):
        wait_for(hp_in.at[k], h_recv.at[k])
        hidden_grad += hp_in[k].astype(jnp.float32)
    normed_grad = hidden_grad * gain_ref[:, at]
    ig_ref[0] = (
        og[...].astype(jnp.float32) + scale_col * (normed_grad - normed * mean)
    ).astype(jnp.bfloat16)

    arrived(gx, g_recv.at[1])
    gains = gx[0] + gx[1] + gx[2] + gx[3]
    for b in range(8):
        gg_ref[:, b * 128 : (b + 1) * 128] = gains[b : b + 1]

    wait_for(de3_in.at[pl.ds(0, 15)], d_recv.at[2, 0])
    de3_in[x * 4 + t] = de3[x * 4 + t]
    for b in range(4):
        summed = de3_in[b * 4].astype(jnp.float32)
        for k in range(1, 4):
            summed += de3_in[b * 4 + k].astype(jnp.float32)
        lines[:, b * HEAD_DIM : (b + 1) * HEAD_DIM] = summed
    for b in range(4):
        for k in range(4):
            eg_ref[:, b * BLOCK + k * HEAD_DIM : b * BLOCK + (k + 1) * HEAD_DIM] = lines[
                pl.ds(k * 4, 4), b * HEAD_DIM : (b + 1) * HEAD_DIM
            ]

    for c in range(len(PIECES)):
        wait_bytes(z_send.at[c], 3 * PIECES[c][3])
    for h in range(HEADS_HERE):
        wait_bytes(x_send.at[h], 12 * SHARD)
        for m in range(2):
            arrived((part.at[0, h], pg.at[h])[m], p_send.at[m, h])
            arrived(dkv.at[m, h], k_send.at[m, h])
    arrived(hg, a_send.at[0])
    wait_for(enc64.at[pl.ds(0, 48)], e_send.at[0])
    wait_for(enc.at[pl.ds(0, 48)], e_send.at[1])
    wait_for(enc.at[pl.ds(0, 192)], e_send.at[2])
    wait_for(enc.at[pl.ds(0, 256)], e_send.at[3])
    for k in range(3):
        wait_for(hp.at[k], h_send.at[k])
    arrived(note, i_send.at[0])
    for b in range(2):
        wait_for(de1.at[b], d_send.at[0, b])
        arrived(de2.at[b], d_send.at[1, b])
    wait_for(de3.at[pl.ds(0, 15)], d_send.at[2, 0])
    arrived(gx, g_send.at[1])
    arrived(gz, g_send.at[0])


def shards(
    section_input, out_grad, head_grad, encoder, norm_gain, query_weight, key_weight, value_weight
):
    low, f32 = jnp.bfloat16, jnp.float32
    hbm = pl.BlockSpec(memory_space=pl.ANY)
    vmem = pl.BlockSpec(memory_space=pltpu.VMEM)
    dma = pltpu.SemaphoreType.DMA
    two = (2, HEADS_HERE)
    return pl.pallas_call(
        kernel,
        out_shape=(
            pltpu.VMEM((1, ROWS, BLOCK), low),
            pltpu.VMEM((4, D), f32),
            pltpu.VMEM((1, BLOCK), f32),
        ),
        in_specs=[hbm, hbm, hbm, vmem, hbm, hbm, hbm, hbm],
        out_specs=(vmem, vmem, vmem),
        scratch_shapes=[
            pltpu.VMEM((HEADS_HERE, D, HEAD_DIM), low),
            pltpu.VMEM(two + (BLOCK, HEAD_DIM), low),
            pltpu.VMEM((ROWS, D), low),
            pltpu.VMEM((1, D), f32),
            pltpu.VMEM((ROWS, BLOCK), low),
            pltpu.VMEM((4, ROWS, COLS), low),
            pltpu.VMEM((16, BLOCK), f32),
            pltpu.VMEM((64, BLOCK), low),
            pltpu.VMEM((4, 16, BLOCK), low),
            pltpu.VMEM((4 * ROWS, BLOCK), low),
            pltpu.VMEM((ROWS, D), low),
            pltpu.VMEM((ROWS, 128), f32),
            pltpu.VMEM(two + (4, ROWS, HEAD_DIM), low),
            pltpu.VMEM((HEADS_HERE, 4, ROWS, HEAD_DIM), low),
            pltpu.VMEM((HEADS_HERE, 4, ROWS, ROWS), low),
            pltpu.VMEM((HEADS_HERE, 4, ROWS, ROWS), low),
            pltpu.VMEM((HEADS_HERE, ROWS, HEAD_DIM), low),
            pltpu.VMEM((HEADS_HERE, ROWS, HEAD_DIM), low),
            pltpu.VMEM((HEADS_HERE, ROWS, ROWS), f32),
            pltpu.VMEM((HEADS_HERE, ROWS, HEAD_DIM), low),
            pltpu.VMEM(two + (4, ROWS, HEAD_DIM), low),
            pltpu.VMEM((4, ROWS, BLOCK), low),
            pltpu.VMEM((4, ROWS, BLOCK), low),
            pltpu.VMEM((2, ROWS, BLOCK), low),
            pltpu.VMEM((4, 16, 128), f32),
            pltpu.VMEM((4, 16, 128), f32),
            pltpu.VMEM((4 * ROWS, BLOCK), f32),
            pltpu.VMEM((2, 4, 4, 16, COLS), low),
            pltpu.VMEM((2, 4, 4, 16, COLS), low),
            pltpu.VMEM((2, 4, 4, 16, COLS), low),
            pltpu.VMEM((2, 4, 4, 16, COLS), low),
            pltpu.VMEM((16, 16, HEAD_DIM), low),
            pltpu.VMEM((16, 16, HEAD_DIM), low),
            pltpu.VMEM((4, 8, 128), f32),
            pltpu.VMEM((4, 8, 128), f32),
            dma((11,)),
            dma((len(PIECES),)),
            dma((HEADS_HERE,)),
            dma((len(PIECES),)),
            dma((len(PIECES),)),
            dma((4, HEADS_HERE)),
            dma((4, HEADS_HERE)),
            dma(two),
            dma(two),
            dma((1,)),
            dma((1,)),
            dma(two),
            dma(two),
            dma((4,)),
            dma((4,)),
            dma((3,)),
            dma((4,)),
            dma((1,)),
            dma((1,)),
            dma((3, 2)),
            dma((3, 2)),
            dma((2,)),
            dma((2,)),
        ],
        compiler_params=pltpu.CompilerParams(
            collective_id=0, has_side_effects=True, vmem_limit_bytes=60 * 1024 * 1024
        ),
        cost_estimate=pl.CostEstimate(
            flops=6 * 2 * ROWS * D * COLS, bytes_accessed=4 * 1024 * 1024, transcendentals=0
        ),
    )(
        section_input, out_grad, head_grad, encoder, norm_gain,
        query_weight, key_weight, value_weight,
    )


def solution(mesh):
    placed = (
        P("pipe", "dp", None),
        P("pipe", "dp", None),
        P("pipe", "dp", "tensor"),
        P(("dp", "pipe", "tensor"), None),
        P("pipe", None),
        P("pipe", "dp", "tensor"),
        P("pipe", "dp", "tensor"),
        P("pipe", "dp", "tensor"),
    )
    return jax.shard_map(
        shards,
        mesh=mesh,
        in_specs=placed,
        out_specs=(
            P("pipe", "dp", "tensor"),
            P(("dp", "pipe", "tensor"), None),
            P("pipe", "tensor"),
        ),
        check_vma=False,
    )
```
